512 devices in a mesh: slide: 8 (over y), seq: 64 (over x, z, core).
Axes of the slice: x: 4, y: 8, z: 8, core: 2. Of those that a mesh axis runs over, the one named last changes fastest.
Arguments:
- tile_embeddings: bfloat16 [131072, 1536], P(('slide', 'seq')), parts along dimension 0, may hold values from -16 to 16
- tile_position: int32 [131072], P(('slide', 'seq')), parts along dimension 0, may hold values from -1 to 8191, as said below
- input_weight: bfloat16 [1536, 768], P('seq'), may hold values from -0.15625 to 0.15625
- attention_weight: bfloat16 [768, 1152], replicated, may hold values from -0.28867513 to 0.28867513
Outputs:
- attended: bfloat16 [65536, 384], P(('slide', 'seq')), parts along dimension 0
The draws below stay inside these ranges and needn't reach their ends.
There are 8 independent parts, one for each index of `slide`. The reference program is written for one: setup_inputs(seed, part) draws one part's arguments, and reference() takes and returns one part's arrays. A program takes and returns all parts, laid end to end along the dimension named above; an argument that names none is the same for every part. Nothing has to cross between parts.
Inputs may be any that keep to these rules, and one draw needn't show every extreme that they name: `tile_position`: every position 0 to 8191 stands in exactly one slot; all other slots hold -1. Among the slots of one device at most 8 hold positions of one owner block (positions with equal p // 128), and every owner block gets exactly 8 from some device.
All inputs are finite; a program needn't handle non-finite values.
Results may differ from the reference program's by a relative error of at most 0.012.
The reference program's roundings to bfloat16 on the way count: a program that leaves them out, or rounds other values in their place, can miss the bound.
Values may be sent and summed in bfloat16 or wider, within the bound.
A program may use at most 64 MiB of HBM per device.

```python
import jax
import jax.numpy as jnp
from jax import lax

E = 1536
D = 768
HEADS = 6
HDIM = 64
TOK_DEV = 128
BRANCHES = 3
TOKENS = 8192
SPAN = 1024
SLOT = 8
N_SEQ = 64


def draw_tile_embeddings(key, part):
    key = jax.random.fold_in(key, 7)
    first_key = jax.random.fold_in(key, 0)
    values = jnp.clip(jax.random.normal(first_key, (2 * TOKENS, E), jnp.float32), -3.5, 3.5)
    return values.astype(jnp.bfloat16)


def draw_attention_weight(key, part):
    key = jax.random.fold_in(key, 5)
    keys_all = jax.random.split(key, 1)
    all_width = HEADS * HDIM
    fan_scale = D ** (-0.5)
    joined = jnp.clip(jax.random.normal(keys_all[0], (D, 3 * all_width), jnp.float32), -4.0, 4.0)
    return (joined * fan_scale).astype(jnp.bfloat16)


def draw_tile_position(key, part):
    key = jax.random.fold_in(key, 11)
    keys_all = jax.random.split(key, 5)
    devices = N_SEQ
    selected_tiles = devices // 2
    half_slot = SLOT // 2
    sources = jax.random.permutation(keys_all[0], devices)
    ranking = jax.random.permutation(keys_all[1], devices)
    shifts = jax.random.randint(keys_all[2], (devices, selected_tiles // 2), half_slot // 2, half_slot + 1)
    shifts = shifts.at[:, 0].set(half_slot)
    owners = jnp.arange(devices)[:, None]
    pair_base = 2 * jnp.arange(selected_tiles // 2)[None, :]
    first_src = sources[(owners + pair_base) % devices]
    second_src = sources[(owners + pair_base + 1) % devices]
    heavier = ranking[first_src] > ranking[second_src]
    first_count = half_slot + jnp.where(heavier, shifts, -shifts)
    counts = jnp.stack([first_count, SLOT - first_count], axis=-1).reshape(devices, selected_tiles)
    starts = jnp.cumsum(counts, axis=1) - counts
    orders = jnp.argsort(jax.random.randint(keys_all[3], (devices, TOK_DEV), 0, 1 << 20) * TOK_DEV + jnp.arange(TOK_DEV)[None, :], axis=1)
    circle = jnp.arange(devices)[:, None, None]
    slot_j = jnp.arange(selected_tiles)[None, :, None]
    slot_t = jnp.arange(SLOT)[None, None, :]
    owner_of = (circle - slot_j) % devices
    is_valid = slot_t < counts[owner_of, slot_j]
    index_in = jnp.minimum(starts[owner_of, slot_j] + slot_t, TOK_DEV - 1)
    position = owner_of * TOK_DEV + orders[owner_of, index_in]
    position = jnp.where(is_valid, position, -1).reshape(devices, selected_tiles * SLOT)
    shuffle = jnp.argsort(jax.random.randint(keys_all[4], (devices, selected_tiles * SLOT), 0, 1 << 20) * (selected_tiles * SLOT) + jnp.arange(selected_tiles * SLOT)[None, :], axis=1)
    position = jnp.take_along_axis(position, shuffle, axis=1)
    return position[jnp.argsort(sources)].reshape(-1).astype(jnp.int32)


def block_scale(own_key, shape, cuts, least, top_value):
    gain, own = 1.0, jax.random.fold_in(own_key, 6)
    for dim, parts in cuts:
        steps = jnp.exp(jax.random.uniform(jax.random.fold_in(own, dim), (parts,), jnp.float32, least / len(cuts), top_value / len(cuts)))
        gain = gain * jnp.repeat(steps, shape[dim] // parts).reshape([-1 if axis == dim else 1 for axis in range(len(shape))])
    return gain


def normal_values(own_key, shape, spread, limit, cuts=(), held_as=jnp.bfloat16):
    gain = block_scale(own_key, shape, cuts, -0.22, 0.18) if cuts else 1.0
    drawn = jax.random.normal(own_key, shape, jnp.float32) * spread * gain
    return jnp.minimum(jnp.maximum(drawn, -limit), limit).astype(held_as)


def setup_inputs(seed: int = 0, part: int = 0) -> dict:
    key_of = jax.random.split(jax.random.key(seed), 5)
    part_splits = jax.random.split(jax.random.fold_in(key_of[4], part), 5)
    return {
        "tile_embeddings": draw_tile_embeddings(jax.random.fold_in(jax.random.fold_in(key_of[4], part), 71), part),
        "tile_position": draw_tile_position(jax.random.fold_in(jax.random.fold_in(key_of[4], part), 71), part),
        "input_weight": normal_values(key_of[2], (E, D), E ** -0.5, 0.15625, ((0, 64),)),
        "attention_weight": draw_attention_weight(jax.random.fold_in(key_of[4], 71), part),
    }


def segment_attention(triple):
    query_rows, key_rows, value_rows = triple
    scores = jnp.dot(query_rows, key_rows.T, preferred_element_type=jnp.float32) * (HDIM ** -0.5)
    row_max = jnp.max(scores, axis=1)
    weights = jnp.exp(scores - row_max[:, None])
    row_total = jnp.sum(weights, axis=1)
    branch_sum = jnp.dot(weights.astype(jnp.bfloat16), value_rows, preferred_element_type=jnp.float32)
    return row_max, row_total, branch_sum


def merge_state(earlier, latest):
    joint_max = jnp.maximum(earlier[0], latest[0])
    keep_scale = jnp.exp(earlier[0] - joint_max)
    take_scale = jnp.exp(latest[0] - joint_max)
    combined_total = earlier[1] * keep_scale + latest[1] * take_scale
    joint_sum = earlier[2] * keep_scale[:, None] + latest[2] * take_scale[:, None]
    return joint_max, combined_total, joint_sum


def strided_rows(matrix, start_row, stride):
    return matrix[start_row::stride].reshape(-1, SPAN, HDIM)


def reference(tile_embeddings, tile_position, input_weight, attention_weight):
    targets = jnp.where(tile_position >= 0, tile_position, TOKENS).astype(jnp.int32)
    placed = jnp.zeros((TOKENS, E), tile_embeddings.dtype).at[targets].set(tile_embeddings, mode="drop")
    sequence = jnp.dot(placed, input_weight, preferred_element_type=jnp.float32).astype(jnp.bfloat16)
    projections = jnp.dot(sequence, attention_weight, preferred_element_type=jnp.float32).astype(jnp.bfloat16)
    all_width = HEADS * HDIM
    outputs = []
    for head_index in range(HEADS):
        first_col = head_index * HDIM
        query_rows = projections[:, first_col:first_col + HDIM]
        key_rows = projections[:, all_width + first_col:all_width + first_col + HDIM]
        value_rows = projections[:, 2 * all_width + first_col:2 * all_width + first_col + HDIM]
        merged = None
        for branch in range(BRANCHES):
            stride = 2 ** branch
            start_row = head_index % stride
            row_max, row_total, branch_sum = lax.map(segment_attention, (strided_rows(query_rows, start_row, stride), strided_rows(key_rows, start_row, stride), strided_rows(value_rows, start_row, stride)))
            latest = (row_max.reshape(-1), row_total.reshape(-1), branch_sum.reshape(-1, HDIM))
            if branch == 0:
                merged = latest
            else:
                earlier = (merged[0][start_row::stride], merged[1][start_row::stride], merged[2][start_row::stride])
                joined = merge_state(earlier, latest)
                merged = (merged[0].at[start_row::stride].set(joined[0]), merged[1].at[start_row::stride].set(joined[1]), merged[2].at[start_row::stride].set(joined[2]))
        outputs.append(merged[2] / merged[1][:, None])
    return jnp.concatenate(outputs, axis=1).astype(jnp.bfloat16)
```

```python
import math

import jax
import jax.numpy as jnp
from jax import lax
from jax.experimental import pallas as pl
from jax.experimental.pallas import tpu as pltpu
from jax.sharding import PartitionSpec as P

E = 1536
D = 768
HALF = 384
TOK_DEV = 128
SLOTS = 256
NX = 4
NZ = 8
W_ROWS = 24
EXP2_SCALE = math.log2(math.e) * 64.0 ** -0.5
MESH = pl.DeviceIdType.MESH
F32 = jnp.float32
BF16 = jnp.bfloat16


def iota(shape, dim):
    return lax.broadcasted_iota(jnp.int32, shape, dim)


def nt_dot(a, b):
    return lax.dot_general(a, b, (((1,), (1,)), ((), ())), preferred_element_type=F32)


def roll64(a):
    return jnp.concatenate([a[:, 64:], a[:, :64]], axis=1)


N_COPIES = 160


def kernel(
    emb_ref, pos_ref, w_ref, aw_ref, out_ref,
    emb_own, emb_sib, pos_sib, w_sib, wbuf, awbuf, awc,
    marks, marks_mid, marks_z, marks_got,
    seq, mid, got, xout, kv, c2, qm, m_s, l_s, acc_s, mask_s, fin, seqh,
    send_sems, recv_sems, local_sems,
):
    me = lax.axis_index("seq")
    slide = lax.axis_index("slide")
    x, z, c = me // 16, (me % 16) // 2, me % 2

    def dev(xx, zz, cc):
        return (slide, xx * 16 + zz * 2 + cc)

    sibling = dev(x, z, 1 - c)
    x_of = [(x + d) % NX for d in range(NX)]
    z_of = [(z + d) % NZ for d in range(NZ)]
    right, left = dev(x, z_of[1], c), dev(x, z_of[7], c)
    x_pair = dev(x + 1 - 2 * (x % 2), z, c)

    started = []

    def remote(src, dst, target):
        k = len(started)
        copy = pltpu.make_async_remote_copy(
            src_ref=src, dst_ref=dst, send_sem=send_sems.at[k], recv_sem=recv_sems.at[k],
            device_id=target, device_id_type=MESH,
        )
        started.append(copy)
        copy.start()
        return copy

    emb_load = pltpu.make_async_copy(emb_ref, emb_own, local_sems.at[0])
    emb_load.start()
    aw_load = pltpu.make_async_copy(aw_ref, awbuf, local_sems.at[1])
    aw_load.start()

    barrier = pltpu.get_barrier_semaphore()
    partners = [sibling] + [dev(x_of[d], z, c) for d in (1, 2, 3)] + [dev(x, z_of[d], c) for d in range(1, 8)]
    for partner in partners:
        pl.semaphore_signal(barrier, inc=1, device_id=partner, device_id_type=MESH)
    pl.semaphore_wait(barrier, len(partners))

    w_copy = remote(w_ref.at[:, pl.ds(pl.multiple_of((1 - c) * HALF, 128), HALF)], w_sib, sibling)
    pos_copy = remote(pos_ref, pos_sib, sibling)
    emb_load.wait()
    emb_copy = remote(emb_own, emb_sib, sibling)

    w_copy.wait_recv()
    w_mine = w_ref[:, pl.ds(pl.multiple_of(c * HALF, 128), HALF)].astype(F32)
    w_theirs = w_sib[...].astype(F32)
    first = jnp.where(c == 0, w_mine, w_theirs)
    second = jnp.where(c == 0, w_theirs, w_mine)
    wbuf[x, z] = jnp.concatenate([first, second], axis=0).astype(BF16)

    w_x = {}
    w_right, w_left = {}, {}
    own_block = wbuf.at[x, z]
    for d in (1, 3, 2):
        w_x[d] = remote(own_block, own_block, dev(x_of[d], z, c))
    w_right[0, 0] = remote(own_block, own_block, right)
    w_left[0, 0] = remote(own_block, own_block, left)

    pos_copy.wait_recv()
    pos = jnp.concatenate([pos_ref[...], pos_sib[...]], axis=1)
    slots = 2 * SLOTS
    lane_t = iota((1, slots), 1)
    owner = pos >> 7
    chip = pos >> 8
    owner_hot = iota((64, slots), 0) == owner
    upper = (iota((slots, slots), 0) < iota((slots, slots), 1)) & (
        (iota((slots, slots), 0) // SLOTS) == (iota((slots, slots), 1) // SLOTS)
    )
    before = jnp.dot(
        owner_hot.astype(F32).astype(BF16), upper.astype(F32).astype(BF16), preferred_element_type=F32
    )
    rank = jnp.sum(jnp.where(owner_hot, before, 0.0), axis=0, keepdims=True)
    source_core = jnp.where(lane_t < SLOTS, c, 1 - c)
    target_row = jnp.where(pos >= 0, (owner * 16 + source_core * 8).astype(F32) + rank, -1.0)
    in_chip = jnp.where(pos >= 0, ((owner % 2) * 16 + source_core * 8).astype(F32) + rank, -1.0)
    chip_hot = (iota((32, slots), 0) == chip).astype(F32).astype(BF16)
    value = ((pos & 255) + 1).astype(F32)
    row_kind = (iota((128, slots), 0) % 32).astype(F32)
    marked = jnp.where(row_kind == in_chip, value, 0.0).astype(BF16)
    marks[...] = nt_dot(chip_hot, marked).reshape(NX, 8, 128)

    mark_x = {}
    for d in (1, 3, 2):
        mark_x[d] = remote(marks.at[x_of[d]], marks_mid.at[x], dev(x_of[d], z, c))

    for d in (1, 3, 2):
        w_x[d].wait_recv()
        xo = (x - d) % NX
        block = wbuf.at[xo, z]
        w_right[0, d] = remote(block, block, right)
        w_left[0, d] = remote(block, block, left)

    for d in (1, 3, 2):
        mark_x[d].wait_recv()
    lane_group = iota((8, 128), 1) // 32
    merged = jnp.where(lane_group == x, marks[x], 0.0)
    for d in (1, 3, 2):
        xo = (x - d) % NX
        merged = merged + jnp.where(lane_group == xo, marks_mid[xo], 0.0)
    for zz in range(NZ):
        marks_z[zz] = jnp.broadcast_to(merged[zz : zz + 1], (8, 128))
    mark_z = {}
    for d in range(1, NZ):
        mark_z[d] = remote(marks_z.at[z_of[d]], marks_got.at[z], dev(x, z_of[d], c))

    aw_load.wait()
    lane = iota((D, 128), 1)

    def pair(group_a, group_b):
        a = awbuf[:, group_a * 128 : group_a * 128 + 128].astype(F32)
        b = awbuf[:, group_b * 128 : group_b * 128 + 128].astype(F32)
        even = jnp.where(lane < 64, a, roll64(b))
        odd = jnp.where(lane < 64, roll64(a), b)
        return jnp.where(c == 0, even, odd).astype(BF16)

    awc[:, 0:128] = pair(0, 2)
    awc[:, 128:256] = pair(1, 1)
    awc[:, 256:384] = pair(3, 5)
    awc[:, 384:512] = pair(6, 8)
    awc[:, 512:640] = pair(4, 7)

    for s in (1, 2, 3):
        for d in (0, 1, 3, 2):
            xo = (x - d) % NX
            w_right[s - 1, d].wait_recv()
            block = wbuf.at[xo, (z - s) % NZ]
            w_right[s, d] = remote(block, block, right)
            if s <= 2:
                w_left[s - 1, d].wait_recv()
                block = wbuf.at[xo, (z + s) % NZ]
                w_left[s, d] = remote(block, block, left)
    for d in (0, 1, 3, 2):
        w_left[2, d].wait_recv()
        w_right[3, d].wait_recv()

    weight = wbuf[...].reshape(E, HALF)
    seq[0:SLOTS] = jnp.dot(emb_own[...], weight, preferred_element_type=F32).astype(BF16)
    emb_copy.wait_recv()
    seq[SLOTS:] = jnp.dot(emb_sib[...], weight, preferred_element_type=F32).astype(BF16)

    out_x = {}
    z_sent = {}

    def rows_for(xo):
        hot = (iota((256, slots), 0) + xo * 256).astype(F32) == target_row
        rows = jnp.dot(hot.astype(F32).astype(BF16), seq[...], preferred_element_type=F32)
        return rows.astype(BF16).reshape(NZ, 32, HALF)

    mid[x] = rows_for(x)
    for d in (4, 3, 5, 2, 6, 1, 7):
        z_sent[0, d] = remote(mid.at[x, z_of[d]], got.at[z, x], dev(x, z_of[d], c))
    for d in (2, 1, 3):
        xout[d - 1] = rows_for(x_of[d])
        out_x[d] = remote(xout.at[d - 1], mid.at[x], dev(x_of[d], z, c))
    for d in (1, 3, 2):
        out_x[d].wait_recv()
        xo = (x - d) % NX
        for e in (4, 3, 5, 2, 6, 1, 7):
            z_sent[d, e] = remote(mid.at[xo, z_of[e]], got.at[z, xo], dev(x, z_of[e], c))

    row = iota((256, 128), 0)
    group = row // 64
    wanted = (((row % 64) // 32) * 128 + (row % 32) * 4 + (group % 2) * 2 + group // 2 + 1).astype(F32)

    def place(zo_marks, rows):
        hot = (zo_marks == wanted).astype(F32).astype(BF16)
        return jnp.dot(hot, rows.reshape(128, HALF), preferred_element_type=F32)

    total = place(marks_z[z][0:1], mid[:, z])
    for d in (1, 7, 2, 6, 3, 5, 4):
        mark_z[d].wait_recv()
        for e in range(NX):
            z_sent[e, d].wait_recv()
        zo = (z - d) % NZ
        total = total + place(marks_got[zo][0:1], got[zo])
    seqh[c] = total.astype(BF16)
    half_copy = remote(seqh.at[c], seqh.at[c], sibling)

    def project(h):
        w = awc[pl.ds(pl.multiple_of(h * HALF, 128), HALF), :]
        return jnp.concatenate([
            jnp.dot(seqh[h, pl.ds(pl.multiple_of(c * 128, 128), 128), :], w, preferred_element_type=F32),
            jnp.dot(seqh[h, pl.ds(pl.multiple_of((1 - c) * 128, 128), 128), :], w, preferred_element_type=F32),
        ], axis=0)

    part = project(c)
    half_copy.wait_recv()
    proj = (part + project(1 - c)).astype(BF16)
    kv[z] = proj[:, 256:640]

    kv_right, kv_left, pair_copies = {}, {}, {}

    def to_pair(name, zo):
        pair_copies[name] = (
            remote(kv.at[zo, 0:64, 0:256], c2.at[zo, :, 0:256], x_pair),
            remote(kv.at[zo, 64:128, 256:384], c2.at[zo, :, 256:384], x_pair),
        )

    kv_right[0] = remote(kv.at[z], kv.at[z], right)
    kv_left[0] = remote(kv.at[z], kv.at[z], left)
    to_pair(0, z)

    lane256 = iota((256, 128), 1)
    q01 = proj[:, 0:128].astype(F32)
    q2 = proj[:, 128:256].astype(F32)
    qm[0] = jnp.where(lane256 < 64, q01, 0.0).astype(BF16)
    qm[1] = jnp.where(lane256 < 64, 0.0, q01).astype(BF16)
    qm[2] = jnp.where(lane256 < 64, q2, 0.0).astype(BF16)

    rr, cc = iota((256, 256), 0), iota((256, 256), 1)
    both = jnp.where((rr < 128) & (cc < 128), 2.0, 1.0)
    mask_s[0] = both + jnp.where((rr < 64) & (cc < 64), 1.0, 0.0)
    mask_s[1] = both + jnp.where((rr >= 64) & (rr < 128) & (cc >= 64) & (cc < 128), 1.0, 0.0)

    key_cols = (0, 0, 256)
    value_cols = (128, 128, 256)

    def update(h, lo, rows, keys, values, mult, fresh=False):
        at = pl.ds(lo, rows)
        s = nt_dot(qm[h, at, :], keys)
        top = jnp.max(s, axis=1, keepdims=True)
        if fresh:
            m_new = top
        else:
            m_old = m_s[h, at, :]
            m_new = jnp.maximum(m_old, top)
            keep = jnp.exp2((m_old - m_new) * EXP2_SCALE)
        p = jnp.exp2((s - m_new) * EXP2_SCALE)
        if mult is not None:
            p = p * mult
        total_p = jnp.sum(p, axis=1, keepdims=True)
        pv = jnp.dot(p.astype(BF16), values, preferred_element_type=F32)
        m_s[h, at, :] = m_new
        if fresh:
            l_s[h, at, :] = total_p
            acc_s[h, at, :] = pv
        else:
            l_s[h, at, :] = l_s[h, at, :] * keep + total_p
            acc_s[h, at, :] = acc_s[h, at, :] * keep + pv

    def full_block(zo, fresh=False):
        for h in range(3):
            update(
                h, 0, 256, kv[zo, :, key_cols[h] : key_cols[h] + 128],
                kv[zo, :, value_cols[h] : value_cols[h] + 128], mask_s[h // 2], fresh,
            )

    def part_block(zo):
        for h in range(3):
            update(
                h, 0, 128, kv[zo, 0:128, key_cols[h] : key_cols[h] + 128],
                kv[zo, 0:128, value_cols[h] : value_cols[h] + 128],
                mask_s[h // 2, 0:128, 0:128] - 1.0,
            )

    def attend(zo):
        same = zo // 4 == z // 4

        @pl.when(same)
        def _():
            full_block(zo)

        @pl.when(jnp.logical_not(same))
        def _():
            part_block(zo)

    full_block(z, fresh=True)
    for s in (1, 2, 3):
        zr, zl = (z - s) % NZ, (z + s) % NZ
        kv_right[s - 1].wait_recv()
        if s < 3:
            kv_right[s] = remote(kv.at[zr], kv.at[zr], right)
        else:
            kv_right[s] = remote(kv.at[zr, 0:128], kv.at[zr, 0:128], right)
        kv_left[s - 1].wait_recv()
        if s < 3:
            kv_left[s] = remote(kv.at[zl], kv.at[zl], left)
        to_pair(("r", s), zr)
        to_pair(("l", s), zl)
        attend(zr)
        attend(zl)
    kv_right[3].wait_recv()
    z_far = (z + 4) % NZ
    to_pair("far", z_far)
    part_block(z_far)
    for copies in pair_copies.values():
        for copy in copies:
            copy.wait_recv()
    for h in range(3):
        update(
            h, 64 * (h // 2), 64,
            c2[:, :, key_cols[h] : key_cols[h] + 128].reshape(512, 128),
            c2[:, :, value_cols[h] : value_cols[h] + 128].reshape(512, 128), None,
        )

    heads = [acc_s[h] / l_s[h] for h in range(3)]
    done = jnp.concatenate(
        [jnp.where(lane256 < 64, heads[0], heads[1]), heads[2]], axis=1
    ).astype(BF16)
    p_row, n_col = iota((128, 256), 0), iota((128, 256), 1)

    def arranged(oc):
        res = p_row % 4
        source = jnp.where(res % 2 == c, 0, 128) + (res // 2) * 64 + oc * 32 + p_row // 4
        hot = (n_col == source).astype(F32).astype(BF16)
        rows = jnp.dot(hot, done, preferred_element_type=F32)
        a, b = rows[:, 0:128], rows[:, 128:256]
        a_rolled, b_rolled = roll64(a), roll64(b)
        return jnp.concatenate([
            jnp.where(c == 0, a, a_rolled),
            jnp.where(c == 0, b_rolled, b),
            jnp.where(c == 0, a_rolled, a),
        ], axis=1)

    fin[0] = arranged(1 - c).astype(BF16)
    fin_copy = remote(fin.at[0], fin.at[1], sibling)
    mine = arranged(c)
    fin_copy.wait_recv()
    own_lane = (iota((128, HALF), 1) // 64) % 2 == c
    out_ref[...] = jnp.where(own_lane, mine, fin[1].astype(F32)).astype(BF16)

    for copy in started:
        copy.wait_send()


def local(tile_embeddings, tile_position, input_weight, attention_weight):
    vmem = pl.BlockSpec(memory_space=pltpu.VMEM)
    anywhere = pl.BlockSpec(memory_space=pl.ANY)
    scratch = [
        pltpu.VMEM((SLOTS, E), BF16),
        pltpu.VMEM((SLOTS, E), BF16),
        pltpu.VMEM((1, SLOTS), jnp.int32),
        pltpu.VMEM((W_ROWS, HALF), BF16),
        pltpu.VMEM((NX, NZ, 2 * W_ROWS, HALF), BF16),
        pltpu.VMEM((D, 1152), BF16),
        pltpu.VMEM((D, 640), BF16),
        pltpu.VMEM((NX, NZ, 128), F32),
        pltpu.VMEM((NX, NZ, 128), F32),
        pltpu.VMEM((NZ, 8, 128), F32),
        pltpu.VMEM((NZ, 8, 128), F32),
        pltpu.VMEM((2 * SLOTS, HALF), BF16),
        pltpu.VMEM((NX, NZ, 32, HALF), BF16),
        pltpu.VMEM((NZ, NX, 32, HALF), BF16),
        pltpu.VMEM((3, NZ, 32, HALF), BF16),
        pltpu.VMEM((NZ, 256, HALF), BF16),
        pltpu.VMEM((NZ, 64, HALF), BF16),
        pltpu.VMEM((3, 256, 128), BF16),
        pltpu.VMEM((3, 256, 1), F32),
        pltpu.VMEM((3, 256, 1), F32),
        pltpu.VMEM((3, 256, 128), F32),
        pltpu.VMEM((2, 256, 256), F32),
        pltpu.VMEM((2, 128, HALF), BF16),
        pltpu.VMEM((2, 256, HALF), BF16),
        pltpu.SemaphoreType.DMA((N_COPIES,)),
        pltpu.SemaphoreType.DMA((N_COPIES,)),
        pltpu.SemaphoreType.DMA((2,)),
    ]
    return pl.pallas_call(
        kernel,
        out_shape=jax.ShapeDtypeStruct((TOK_DEV, HALF), BF16),
        in_specs=[anywhere, vmem, vmem, anywhere],
        out_specs=vmem,
        scratch_shapes=scratch,
        compiler_params=pltpu.CompilerParams(
            collective_id=0, has_side_effects=True, vmem_limit_bytes=48 * 1024 * 1024
        ),
    )(tile_embeddings, tile_position.reshape(1, SLOTS), input_weight, attention_weight)


def solution(mesh):
    in_specs = (P(("slide", "seq"), None), P(("slide", "seq")), P("seq", None), P())
    out_specs = P(("slide", "seq"), None)
    return jax.shard_map(local, mesh=mesh, in_specs=in_specs, out_specs=out_specs, check_vma=False)
```

```python
import math

import jax
import jax.numpy as jnp
from jax import lax
from jax.experimental import pallas as pl
from jax.experimental.pallas import tpu as pltpu
from jax.sharding import PartitionSpec as P

E = 1536
D = 768
HALF = 384
TOK_DEV = 128
SLOTS = 256
NX = 4
NZ = 8
W_ROWS = 24
EXP2_SCALE = math.log2(math.e) * 64.0 ** -0.5
MESH = pl.DeviceIdType.MESH
F32 = jnp.float32
BF16 = jnp.bfloat16


def iota(shape, dim):
    return lax.broadcasted_iota(jnp.int32, shape, dim)


def nt_dot(a, b):
    return lax.dot_general(a, b, (((1,), (1,)), ((), ())), preferred_element_type=F32)


def roll64(a):
    return jnp.concatenate([a[:, 64:], a[:, :64]], axis=1)


N_COPIES = 230
N_W = 70


def kernel(
    emb_in, pos_in, w_in, aw_in, out_ref,
    pos_ref, w_ref,
    emb_own, emb_sib, pos_sib, wbuf, awbuf, awc,
    marks, marks_mid, marks_z, marks_got,
    hot_s, seq, mid, got, xout, kv, c2, qm, m_s, l_s, acc_s, mask_s, fin, seqh,
    send_sems, recv_sems, w_sems, local_sems,
):
    me = lax.axis_index("seq")
    slide = lax.axis_index("slide")
    x, z, c = me // 16, (me % 16) // 2, me % 2

    def dev(xx, zz, cc):
        return (slide, xx * 16 + zz * 2 + cc)

    sibling = dev(x, z, 1 - c)
    x_of = [(x + d) % NX for d in range(NX)]
    z_of = [(z + d) % NZ for d in range(NZ)]
    right, left = dev(x, z_of[1], c), dev(x, z_of[7], c)
    x_pair = dev(x + 1 - 2 * (x % 2), z, c)

    started = []
    w_names = {}

    def remote(src, dst, target, when=None, recv_sem=None):
        k = len(started)
        copy = pltpu.make_async_remote_copy(
            src_ref=src, dst_ref=dst, send_sem=send_sems.at[k],
            recv_sem=recv_sems.at[k] if recv_sem is None else recv_sem,
            device_id=target, device_id_type=MESH,
        )
        started.append((copy, when))
        if when is None:
            copy.start()
        else:
            pl.when(when)(copy.start)
        return copy

    w_load = pltpu.make_async_copy(w_in, w_ref, local_sems.at[0])
    pos_load = pltpu.make_async_copy(pos_in, pos_ref, local_sems.at[1])
    emb_load = pltpu.make_async_copy(emb_in, emb_own, local_sems.at[2])
    aw_load = pltpu.make_async_copy(aw_in, awbuf, local_sems.at[3])
    for load in (w_load, pos_load, emb_load, aw_load):
        load.start()

    barrier = pltpu.get_barrier_semaphore()
    partners = [sibling] + [dev(x_of[d], z, c) for d in (1, 2, 3)] + [dev(x, z_of[d], c) for d in range(1, 8)]
    partners += [dev(x_of[d], z, 1 - c) for d in (1, 2, 3)] + [dev(x, z_of[d], 1 - c) for d in (1, 4, 7)]
    for partner in partners:
        pl.semaphore_signal(barrier, inc=1, device_id=partner, device_id_type=MESH)
    pl.semaphore_wait(barrier, len(partners))

    w_load.wait()

    def w_half(h):
        return w_ref.at[:, pl.ds(pl.multiple_of(h * HALF, 128), HALF)]

    own_slot = wbuf.at[x, z, c]

    def w_sem(name, core):
        k = w_names.setdefault(name, len(w_names))
        return w_sems.at[2 * k + core]

    def w_give(name, target_x, target_z, when=None):
        for half in (c, 1 - c):
            remote(w_half(half), own_slot, dev(target_x, target_z, half), when, w_sem(name, c))

    def w_take(name, xo, zo, core):
        slot = wbuf.at[xo, zo, core]
        pltpu.make_async_remote_copy(
            src_ref=slot, dst_ref=slot, send_sem=send_sems.at[0], recv_sem=w_sem(name, core),
            device_id=sibling, device_id_type=MESH,
        ).wait_recv()
        return slot

    w_give(("z", 1), x, z_of[1])
    w_give(("z", 7), x, z_of[7])
    w_give(("z", 4), x, z_of[4], c == 1)
    for d in (1, 3, 2):
        w_give(("x", d), x_of[d], z)
    remote(w_half(1 - c), own_slot, sibling, None, w_sem("cross", c))
    pos_load.wait()
    pos_copy = remote(pos_ref, pos_sib, sibling)
    emb_load.wait()
    emb_copy = remote(emb_own, emb_sib, sibling)
    wbuf[x, z, c] = w_ref[:, pl.ds(pl.multiple_of(c * HALF, 128), HALF)]

    def w_send(name, slot, xx, zz, core):
        remote(slot, slot, dev(xx, zz, c), None, w_sem(name, core))

    def w_along_x(e, slot):
        for d in (1, 3, 2):
            w_send(("zx", e, d), slot, x_of[d], z, 1)

    def w_ring(way, s, d):
        if s == 0 and d == 0:
            return ("z", 1) if way == 0 else ("z", 7)
        return ("ring", way, s, d)

    def w_ring_step(s):
        for d in (0, 1, 3, 2):
            xo = (x - d) % NX
            for way in (0, 1):
                if s > (4, 3)[way]:
                    continue
                zo = (z - s) % NZ if way == 0 else (z + s) % NZ
                slot = w_take(w_ring(way, s - 1, d), xo, zo, 0)
                if s < (4, 3)[way]:
                    w_send(w_ring(way, s, d), slot, x, z_of[(1, 7)[way]], 0)

    aw_load.wait()
    lane = iota((D, 128), 1)

    def pair(group_a, group_b):
        a = awbuf[:, group_a * 128 : group_a * 128 + 128].astype(F32)
        b = awbuf[:, group_b * 128 : group_b * 128 + 128].astype(F32)
        even = jnp.where(lane < 64, a, roll64(b))
        odd = jnp.where(lane < 64, roll64(a), b)
        return jnp.where(c == 0, even, odd).astype(BF16)

    awc[:, 0:128] = pair(0, 2)
    awc[:, 128:256] = pair(1, 1)
    awc[:, 256:384] = pair(3, 5)
    awc[:, 384:512] = pair(6, 8)
    awc[:, 512:640] = pair(4, 7)

    for d in (1, 3, 2):
        xo = (x - d) % NX
        slot = w_take(("x", d), xo, z, 0)
        for way in (0, 1):
            w_send(w_ring(way, 0, d), slot, x, z_of[(1, 7)[way]], 0)
    for e, onward in ((1, ((7, 2),)), (7, ((1, 6),)), (4, ((1, 3), (7, 5)))):
        slot = w_take(("z", 8 - e), x, z_of[e], 1)
        for to, seen in onward:
            w_send(("far", seen), slot, x, z_of[to], 1)
        w_along_x(e, slot)

    pos_copy.wait_recv()
    pos = jnp.concatenate([pos_ref[...], pos_sib[...]], axis=1)
    slots = 2 * SLOTS
    lane_t = iota((1, slots), 1)
    owner = pos >> 7
    chip = pos >> 8
    owner_hot = iota((64, slots), 0) == owner
    upper = (iota((slots, slots), 0) < iota((slots, slots), 1)) & (
        (iota((slots, slots), 0) // SLOTS) == (iota((slots, slots), 1) // SLOTS)
    )
    before = jnp.dot(
        owner_hot.astype(F32).astype(BF16), upper.astype(F32).astype(BF16), preferred_element_type=F32
    )
    rank = jnp.sum(jnp.where(owner_hot, before, 0.0), axis=0, keepdims=True)
    source_core = jnp.where(lane_t < SLOTS, c, 1 - c)
    target_row = jnp.where(pos >= 0, (owner * 16 + source_core * 8).astype(F32) + rank, -1.0)
    in_chip = jnp.where(pos >= 0, ((owner % 2) * 16 + source_core * 8).astype(F32) + rank, -1.0)
    chip_hot = (iota((32, slots), 0) == chip).astype(F32).astype(BF16)
    value = ((pos & 255) + 1).astype(F32)
    row_kind = (iota((128, slots), 0) % 32).astype(F32)
    marked = jnp.where(row_kind == in_chip, value, 0.0).astype(BF16)
    marks[...] = nt_dot(chip_hot, marked).reshape(NX, 8, 128)

    mark_x = {}
    for d in (1, 3, 2):
        mark_x[d] = remote(marks.at[x_of[d]], marks_mid.at[x], dev(x_of[d], z, c))

    w_ring_step(1)
    for e in (2, 6, 3, 5):
        w_along_x(e, w_take(("far", e), x, z_of[e], 1))

    for d in (1, 3, 2):
        mark_x[d].wait_recv()
    lane_group = iota((8, 128), 1) // 32
    merged = jnp.where(lane_group == x, marks[x], 0.0)
    for d in (1, 3, 2):
        xo = (x - d) % NX
        merged = merged + jnp.where(lane_group == xo, marks_mid[xo], 0.0)
    for zz in range(NZ):
        marks_z[zz] = jnp.broadcast_to(merged[zz : zz + 1], (8, 128))
    mark_z = {}
    for d in range(1, NZ):
        mark_z[d] = remote(marks_z.at[z_of[d]], marks_got.at[z], dev(x, z_of[d], c))

    for d in range(NX):
        rows = iota((256, slots), 0) + x_of[d] * 256
        hot_s[d] = (rows.astype(F32) == target_row).astype(F32).astype(BF16)

    for s in (2, 3, 4):
        w_ring_step(s)
    w_take("cross", x, z, 1 - c)
    for d in (1, 3, 2):
        w_take(("x", d), (x - d) % NX, z, 1)
        for e in range(1, NZ):
            w_take(("zx", e, d), (x - d) % NX, z_of[e], 1)

    weight = wbuf[...].reshape(E, HALF)
    seq[0:SLOTS] = jnp.dot(emb_own[...], weight, preferred_element_type=F32).astype(BF16)
    emb_copy.wait_recv()
    seq[SLOTS:] = jnp.dot(emb_sib[...], weight, preferred_element_type=F32).astype(BF16)

    out_x = {}
    z_sent = {}

    def rows_for(d):
        rows = jnp.dot(hot_s[d], seq[...], preferred_element_type=F32)
        return rows.astype(BF16).reshape(NZ, 32, HALF)

    def send_x(d):
        xout[d - 1] = rows_for(d)
        out_x[d] = remote(xout.at[d - 1], mid.at[x], dev(x_of[d], z, c))

    def send_z(d):
        xo = (x - d) % NX
        for e in (4, 3, 5, 2, 6, 1, 7):
            z_sent[d, e] = remote(mid.at[xo, z_of[e]], got.at[z, xo], dev(x, z_of[e], c))

    send_x(1)
    send_x(3)
    mid[x] = rows_for(0)
    send_z(0)
    send_x(2)
    for d in (1, 3, 2):
        out_x[d].wait_recv()
        send_z(d)

    row = iota((256, 128), 0)
    group = row // 64
    wanted = (((row % 64) // 32) * 128 + (row % 32) * 4 + (group % 2) * 2 + group // 2 + 1).astype(F32)

    def place(zo_marks, rows):
        hot = (zo_marks == wanted).astype(F32).astype(BF16)
        return jnp.dot(hot, rows.reshape(128, HALF), preferred_element_type=F32)

    total = place(marks_z[z][0:1], mid[:, z])
    for d in (1, 7, 2, 6, 3, 5, 4):
        mark_z[d].wait_recv()
        for e in range(NX):
            z_sent[e, d].wait_recv()
        zo = (z - d) % NZ
        total = total + place(marks_got[zo][0:1], got[zo])
    seqh[c] = total.astype(BF16)
    half_copy = remote(seqh.at[c], seqh.at[c], sibling)

    def project(h):
        w = awc[pl.ds(pl.multiple_of(h * HALF, 128), HALF), :]
        return jnp.concatenate([
            jnp.dot(seqh[h, pl.ds(pl.multiple_of(c * 128, 128), 128), :], w, preferred_element_type=F32),
            jnp.dot(seqh[h, pl.ds(pl.multiple_of((1 - c) * 128, 128), 128), :], w, preferred_element_type=F32),
        ], axis=0)

    part = project(c)
    half_copy.wait_recv()
    proj = (part + project(1 - c)).astype(BF16)
    kv[z] = proj[:, 256:640]

    in_seg = (z % 4, 3 - z % 4)
    pair_copies = []
    flow = {}

    def low_sent(i, s):
        return None if s < 3 else (i == 3) | (i == 0)

    def low_got(i, s):
        return None if s < 3 else (i == 0) | (i == 1)

    def rest_sent(i, s):
        return (i >= s) & (i <= 2)

    def rest_got(i, s):
        return i >= s + 1

    def origin(way, s):
        return (z - s) % NZ if way == 0 else (z + s) % NZ

    def pass_on(way, part, s, k):
        sent = low_sent if part == "low" else rest_sent
        block = kv.at[origin(way, s), pl.ds(k * 64 + (0 if part == "low" else 128), 64)]
        flow[way, part, s, k] = remote(block, block, (right, left)[way], sent(in_seg[way], s))

    def wait_for(copy, when):
        if when is None:
            copy.wait_recv()
        else:
            pl.when(when)(copy.wait_recv)

    def to_pair(zo, when=None):
        for rows, cols in ((0, slice(0, 256)), (64, slice(256, 384))):
            copy = remote(kv.at[zo, rows : rows + 64, cols], c2.at[zo, :, cols], x_pair, when)
            pair_copies.append((copy, when))

    for part in ("low", "rest"):
        for k in (0, 1):
            for way in (0, 1):
                pass_on(way, part, 0, k)
    to_pair(z)

    lane256 = iota((256, 128), 1)
    q01 = proj[:, 0:128].astype(F32)
    q2 = proj[:, 128:256].astype(F32)
    qm[0] = jnp.where(lane256 < 64, q01, 0.0).astype(BF16)
    qm[1] = jnp.where(lane256 < 64, 0.0, q01).astype(BF16)
    qm[2] = jnp.where(lane256 < 64, q2, 0.0).astype(BF16)

    rr, cc = iota((256, 256), 0), iota((256, 256), 1)
    both = jnp.where((rr < 128) & (cc < 128), 2.0, 1.0)
    mask_s[0] = both + jnp.where((rr < 64) & (cc < 64), 1.0, 0.0)
    mask_s[1] = both + jnp.where((rr >= 64) & (rr < 128) & (cc >= 64) & (cc < 128), 1.0, 0.0)

    key_cols = (0, 0, 256)
    value_cols = (128, 128, 256)

    def update(h, lo, rows, keys, values, mult, fresh=False):
        at = pl.ds(lo, rows)
        s = nt_dot(qm[h, at, :], keys)
        top = jnp.max(s, axis=1, keepdims=True)
        if fresh:
            m_new = top
        else:
            m_old = m_s[h, at, :]
            m_new = jnp.maximum(m_old, top)
            keep = jnp.exp2((m_old - m_new) * EXP2_SCALE)
        p = jnp.exp2((s - m_new) * EXP2_SCALE)
        if mult is not None:
            p = p * mult
        total_p = jnp.sum(p, axis=1, keepdims=True)
        pv = jnp.dot(p.astype(BF16), values, preferred_element_type=F32)
        m_s[h, at, :] = m_new
        if fresh:
            l_s[h, at, :] = total_p
            acc_s[h, at, :] = pv
        else:
            l_s[h, at, :] = l_s[h, at, :] * keep + total_p
            acc_s[h, at, :] = acc_s[h, at, :] * keep + pv

    def full_block(zo, fresh=False):
        for h in range(3):
            update(
                h, 0, 256, kv[zo, :, key_cols[h] : key_cols[h] + 128],
                kv[zo, :, value_cols[h] : value_cols[h] + 128], mask_s[h // 2], fresh,
            )

    def part_block(zo):
        for h in range(3):
            update(
                h, 0, 128, kv[zo, 0:128, key_cols[h] : key_cols[h] + 128],
                kv[zo, 0:128, value_cols[h] : value_cols[h] + 128],
                mask_s[h // 2, 0:128, 0:128] - 1.0,
            )

    def pair_block(copies, offsets):
        for copy, when in copies:
            wait_for(copy, when)
        blocks = [c2[z_of[e]] for e in offsets]
        block = jnp.concatenate(blocks, axis=0)
        for h in range(3):
            update(
                h, 64 * (h // 2), 64, block[:, key_cols[h] : key_cols[h] + 128],
                block[:, value_cols[h] : value_cols[h] + 128], None,
            )

    full_block(z, fresh=True)
    for s in range(4):
        for k in (0, 1):
            for way in (0, 1):
                wait_for(flow[way, "low", s, k], low_got(in_seg[way], s))
                if s < 3:
                    pass_on(way, "low", s + 1, k)
        for way in (0, 1):
            to_pair(origin(way, s + 1), low_got(in_seg[way], s))
        if s < 3:
            for k in (0, 1):
                for way in (0, 1):
                    pl.when(rest_got(in_seg[way], s))(flow[way, "rest", s, k].wait_recv)
                    if s < 2:
                        pass_on(way, "rest", s + 1, k)
        if s == 3:
            pair_block(pair_copies[:10], (0, 7, 1, 6, 2))
        for way in (0, 1):
            zo = origin(way, s + 1)
            got_low = low_got(in_seg[way], s)
            if s < 3:
                full = rest_got(in_seg[way], s)
                pl.when(full)(lambda: full_block(zo))
                part = jnp.logical_not(full)
                pl.when(part if got_low is None else part & got_low)(lambda: part_block(zo))
            else:
                pl.when(got_low)(lambda: part_block(zo))
    pair_block(pair_copies[10:], (3, 5, 4))

    heads = [acc_s[h] / l_s[h] for h in range(3)]
    done = jnp.concatenate(
        [jnp.where(lane256 < 64, heads[0], heads[1]), heads[2]], axis=1
    ).astype(BF16)
    p_row, n_col = iota((128, 256), 0), iota((128, 256), 1)

    def arranged(oc):
        res = p_row % 4
        source = jnp.where(res % 2 == c, 0, 128) + (res // 2) * 64 + oc * 32 + p_row // 4
        hot = (n_col == source).astype(F32).astype(BF16)
        rows = jnp.dot(hot, done, preferred_element_type=F32)
        a, b = rows[:, 0:128], rows[:, 128:256]
        a_rolled, b_rolled = roll64(a), roll64(b)
        return jnp.concatenate([
            jnp.where(c == 0, a, a_rolled),
            jnp.where(c == 0, b_rolled, b),
            jnp.where(c == 0, a_rolled, a),
        ], axis=1)

    fin[0] = arranged(1 - c).astype(BF16)
    fin_copy = remote(fin.at[0], fin.at[1], sibling)
    mine = arranged(c)
    fin_copy.wait_recv()
    own_lane = (iota((128, HALF), 1) // 64) % 2 == c
    out_ref[...] = jnp.where(own_lane, mine, fin[1].astype(F32)).astype(BF16)

    for copy, when in started:
        if when is None:
            copy.wait_send()
        else:
            pl.when(when)(copy.wait_send)


def local(tile_embeddings, tile_position, input_weight, attention_weight):
    vmem = pl.BlockSpec(memory_space=pltpu.VMEM)
    anywhere = pl.BlockSpec(memory_space=pl.ANY)
    scratch = [
        pltpu.VMEM((1, SLOTS), jnp.int32),
        pltpu.VMEM((W_ROWS, 2 * HALF), BF16),
        pltpu.VMEM((SLOTS, E), BF16),
        pltpu.VMEM((SLOTS, E), BF16),
        pltpu.VMEM((1, SLOTS), jnp.int32),
        pltpu.VMEM((NX, NZ, 2, W_ROWS, HALF), BF16),
        pltpu.VMEM((D, 1152), BF16),
        pltpu.VMEM((D, 640), BF16),
        pltpu.VMEM((NX, NZ, 128), F32),
        pltpu.VMEM((NX, NZ, 128), F32),
        pltpu.VMEM((NZ, 8, 128), F32),
        pltpu.VMEM((NZ, 8, 128), F32),
        pltpu.VMEM((NX, 256, 2 * SLOTS), BF16),
        pltpu.VMEM((2 * SLOTS, HALF), BF16),
        pltpu.VMEM((NX, NZ, 32, HALF), BF16),
        pltpu.VMEM((NZ, NX, 32, HALF), BF16),
        pltpu.VMEM((3, NZ, 32, HALF), BF16),
        pltpu.VMEM((NZ, 256, HALF), BF16),
        pltpu.VMEM((NZ, 64, HALF), BF16),
        pltpu.VMEM((3, 256, 128), BF16),
        pltpu.VMEM((3, 256, 1), F32),
        pltpu.VMEM((3, 256, 1), F32),
        pltpu.VMEM((3, 256, 128), F32),
        pltpu.VMEM((2, 256, 256), F32),
        pltpu.VMEM((2, 128, HALF), BF16),
        pltpu.VMEM((2, 256, HALF), BF16),
        pltpu.SemaphoreType.DMA((N_COPIES,)),
        pltpu.SemaphoreType.DMA((N_COPIES,)),
        pltpu.SemaphoreType.DMA((2 * N_W,)),
        pltpu.SemaphoreType.DMA((4,)),
    ]
    return pl.pallas_call(
        kernel,
        out_shape=jax.ShapeDtypeStruct((TOK_DEV, HALF), BF16),
        in_specs=[anywhere] * 4,
        out_specs=vmem,
        scratch_shapes=scratch,
        compiler_params=pltpu.CompilerParams(
            collective_id=0, has_side_effects=True, vmem_limit_bytes=60 * 1024 * 1024
        ),
    )(tile_embeddings, tile_position.reshape(1, SLOTS), input_weight, attention_weight)


def solution(mesh):
    in_specs = (P(("slide", "seq"), None), P(("slide", "seq")), P("seq", None), P())
    out_specs = P(("slide", "seq"), None)
    return jax.shard_map(local, mesh=mesh, in_specs=in_specs, out_specs=out_specs, check_vma=False)
```

```python
import math

import jax
import jax.numpy as jnp
from jax import lax
from jax.experimental import pallas as pl
from jax.experimental.pallas import tpu as pltpu
from jax.sharding import PartitionSpec as P

E = 1536
D = 768
HALF = 384
TOK_DEV = 128
SLOTS = 256
NX = 4
NZ = 8
W_ROWS = 24
EXP2_SCALE = math.log2(math.e) * 64.0 ** -0.5
MESH = pl.DeviceIdType.MESH
F32 = jnp.float32
BF16 = jnp.bfloat16


def iota(shape, dim):
    return lax.broadcasted_iota(jnp.int32, shape, dim)


def nt_dot(a, b):
    return lax.dot_general(a, b, (((1,), (1,)), ((), ())), preferred_element_type=F32)


def roll64(a):
    return jnp.concatenate([a[:, 64:], a[:, :64]], axis=1)


N_SEMS = 100


def kernel(
    emb_in, pos_in, w_in, aw_in, out_ref,
    pos_ref, w_ref,
    emb_own, emb_sib, pos_sib, wbuf, awbuf, awc,
    marks, marks_mid, marks_z, marks_got,
    hot_s, seq, mid, got, xout, kv, c2, qm, m_s, l_s, acc_s, mask_s, fin, seqh,
    sems, local_sems,
):
    me = lax.axis_index("seq")
    slide = lax.axis_index("slide")
    x, z, c = me // 16, (me % 16) // 2, me % 2

    def dev(xx, zz, cc):
        return (slide, xx * 16 + zz * 2 + cc)

    sibling = dev(x, z, 1 - c)
    x_of = [(x + d) % NX for d in range(NX)]
    z_of = [(z + d) % NZ for d in range(NZ)]
    right, left = dev(x, z_of[1], c), dev(x, z_of[7], c)
    x_pair = dev(x + 1 - 2 * (x % 2), z, c)

    names = {}

    def sem(name):
        return sems.at[names.setdefault(name, len(names))]

    def guarded(when, action):
        if when is None:
            action()
        else:
            pl.when(when)(action)

    def put(src, dst, target, sent_as, got_as, when=None):
        copy = pltpu.make_async_remote_copy(
            src_ref=src, dst_ref=dst, send_sem=sem(("sent", sent_as)), recv_sem=sem(got_as),
            device_id=target, device_id_type=MESH,
        )
        guarded(when, copy.start)

    def bytes_of(ref, name):
        return pltpu.make_async_remote_copy(
            src_ref=ref, dst_ref=ref, send_sem=sem(name), recv_sem=sem(name),
            device_id=sibling, device_id_type=MESH,
        )

    def take(ref, name, when=None):
        guarded(when, bytes_of(ref, name).wait_recv)
        return ref

    def sent(ref, name, when=None):
        guarded(when, bytes_of(ref, ("sent", name)).wait_send)

    w_load = pltpu.make_async_copy(w_in, w_ref, local_sems.at[0])
    pos_load = pltpu.make_async_copy(pos_in, pos_ref, local_sems.at[1])
    emb_load = pltpu.make_async_copy(emb_in, emb_own, local_sems.at[2])
    aw_load = pltpu.make_async_copy(aw_in, awbuf, local_sems.at[3])
    for load in (w_load, pos_load, emb_load, aw_load):
        load.start()

    barrier = pltpu.get_barrier_semaphore()
    partners = [sibling] + [dev(x_of[d], z, c) for d in (1, 2, 3)] + [dev(x, z_of[d], c) for d in range(1, 8)]
    partners += [dev(x_of[d], z, 1 - c) for d in (1, 2, 3)] + [dev(x, z_of[d], 1 - c) for d in (1, 4, 7)]
    for partner in partners:
        pl.semaphore_signal(barrier, inc=1, device_id=partner, device_id_type=MESH)
    pl.semaphore_wait(barrier, len(partners))

    w_load.wait()

    def w_half(h):
        return w_ref.at[:, pl.ds(pl.multiple_of(h * HALF, 128), HALF)]

    own_slot = wbuf.at[x, z, c]

    def w_give(kind, d, target_x, target_z):
        for half in (c, 1 - c):
            put(w_half(half), own_slot, dev(target_x, target_z, half), kind, (kind, d))

    for d in (4, 1, 7):
        w_give("z", d, x, z_of[d])
    for d in (1, 3, 2):
        w_give("x", d, x_of[d], z)
    put(w_half(1 - c), own_slot, sibling, "cross", "cross")
    pos_load.wait()
    put(pos_ref, pos_sib, sibling, "pos", "pos")
    emb_load.wait()
    put(emb_own, emb_sib, sibling, "emb", "emb")
    wbuf[x, z, c] = w_ref[:, pl.ds(pl.multiple_of(c * HALF, 128), HALF)]

    onward = {1: ((7, 2),), 7: ((1, 6),), 4: ((1, 3), (7, 5))}

    def w_pass_z(kind, slot, e, name):
        for to, seen in onward[e]:
            put(slot, slot, dev(x, z_of[to], c), kind, name(seen))

    def w_along_x(e):
        piece = wbuf.at[x, z_of[e], 1]
        for d in (1, 3, 2):
            put(piece, piece, dev(x_of[d], z, c), "bx", ("bx", d))

    def w_from_z(e):
        slot = take(wbuf.at[x, z_of[e]], ("z", 8 - e))
        w_pass_z("far", slot, e, lambda seen: ("far", seen))
        w_along_x(e)

    aw_load.wait()
    lane = iota((D, 128), 1)

    def pair(group_a, group_b):
        a = awbuf[:, group_a * 128 : group_a * 128 + 128].astype(F32)
        b = awbuf[:, group_b * 128 : group_b * 128 + 128].astype(F32)
        even = jnp.where(lane < 64, a, roll64(b))
        odd = jnp.where(lane < 64, roll64(a), b)
        return jnp.where(c == 0, even, odd).astype(BF16)

    awc[:, 0:128] = pair(0, 2)
    awc[:, 128:256] = pair(1, 1)
    awc[:, 256:384] = pair(3, 5)
    awc[:, 384:512] = pair(6, 8)
    awc[:, 512:640] = pair(4, 7)

    w_from_z(1)
    w_from_z(7)
    for d in (1, 3, 2):
        xo = (x - d) % NX
        take(wbuf.at[xo, z], ("x", d))
        piece = wbuf.at[xo, z, 0]
        for to in (4, 1, 7):
            put(piece, piece, dev(x, z_of[to], c), "az", ("az", to, d))
    w_from_z(4)

    take(pos_sib, "pos")
    pos = jnp.concatenate([pos_ref[...], pos_sib[...]], axis=1)
    slots = 2 * SLOTS
    lane_t = iota((1, slots), 1)
    owner = pos >> 7
    chip = pos >> 8
    owner_hot = iota((64, slots), 0) == owner
    upper = (iota((slots, slots), 0) < iota((slots, slots), 1)) & (
        (iota((slots, slots), 0) // SLOTS) == (iota((slots, slots), 1) // SLOTS)
    )
    before = jnp.dot(
        owner_hot.astype(F32).astype(BF16), upper.astype(F32).astype(BF16), preferred_element_type=F32
    )
    rank = jnp.sum(jnp.where(owner_hot, before, 0.0), axis=0, keepdims=True)
    source_core = jnp.where(lane_t < SLOTS, c, 1 - c)
    target_row = jnp.where(pos >= 0, (owner * 16 + source_core * 8).astype(F32) + rank, -1.0)
    in_chip = jnp.where(pos >= 0, ((owner % 2) * 16 + source_core * 8).astype(F32) + rank, -1.0)
    chip_hot = (iota((32, slots), 0) == chip).astype(F32).astype(BF16)
    value = ((pos & 255) + 1).astype(F32)
    row_kind = (iota((128, slots), 0) % 32).astype(F32)
    marked = jnp.where(row_kind == in_chip, value, 0.0).astype(BF16)
    marks[...] = nt_dot(chip_hot, marked).reshape(NX, 8, 128)

    for d in (1, 3, 2):
        put(marks.at[x_of[d]], marks_mid.at[x], dev(x_of[d], z, c), "mark x", "mark x")

    for e in (2, 6, 3, 5):
        take(wbuf.at[x, z_of[e]], ("far", e))
        w_along_x(e)
    for d in (1, 3, 2):
        xo = (x - d) % NX
        for e in (1, 7, 4):
            piece = take(wbuf.at[xo, z_of[e], 0], ("az", 8 - e, d))
            w_pass_z("afar", piece, e, lambda seen: ("afar", seen))

    take(marks_mid.at[0:3], "mark x")
    lane_group = iota((8, 128), 1) // 32
    merged = jnp.where(lane_group == x, marks[x], 0.0)
    for d in (1, 3, 2):
        xo = (x - d) % NX
        merged = merged + jnp.where(lane_group == xo, marks_mid[xo], 0.0)
    for zz in range(NZ):
        marks_z[zz] = jnp.broadcast_to(merged[zz : zz + 1], (8, 128))
    for d in range(1, NZ):
        put(marks_z.at[z_of[d]], marks_got.at[z], dev(x, z_of[d], c), "mark z", "mark z")

    for d in range(NX):
        rows = iota((256, slots), 0) + x_of[d] * 256
        hot_s[d] = (rows.astype(F32) == target_row).astype(F32).astype(BF16)

    take(wbuf.at[x, z, 1 - c], "cross")
    for d in (1, 3, 2):
        take(wbuf.at[(x - d) % NX, 0:7, 1], ("bx", d))
    for e in (2, 6, 3, 5):
        take(wbuf.at[0:3, z_of[e], 0], ("afar", e))

    weight = wbuf[...].reshape(E, HALF)
    seq[0:SLOTS] = jnp.dot(emb_own[...], weight, preferred_element_type=F32).astype(BF16)
    take(emb_sib, "emb")
    seq[SLOTS:] = jnp.dot(emb_sib[...], weight, preferred_element_type=F32).astype(BF16)

    def rows_for(d):
        rows = jnp.dot(hot_s[d], seq[...], preferred_element_type=F32)
        return rows.astype(BF16).reshape(NZ, 32, HALF)

    def send_x(d):
        xout[d - 1] = rows_for(d)
        put(xout.at[d - 1], mid.at[x], dev(x_of[d], z, c), "out x", ("out x", d))

    def send_z(d):
        xo = (x - d) % NX
        for e in (4, 3, 5, 2, 6, 1, 7):
            put(mid.at[xo, z_of[e]], got.at[z, xo], dev(x, z_of[e], c), "out z", ("out z", e))

    send_x(1)
    send_x(3)
    mid[x] = rows_for(0)
    send_z(0)
    send_x(2)
    for d in (1, 3, 2):
        take(mid.at[(x - d) % NX], ("out x", d))
        send_z(d)

    row = iota((256, 128), 0)
    group = row // 64
    wanted = (((row % 64) // 32) * 128 + (row % 32) * 4 + (group % 2) * 2 + group // 2 + 1).astype(F32)

    def place(zo_marks, rows):
        hot = (zo_marks == wanted).astype(F32).astype(BF16)
        return jnp.dot(hot, rows.reshape(128, HALF), preferred_element_type=F32)

    total = place(marks_z[z][0:1], mid[:, z])
    take(marks_got.at[0:7], "mark z")
    for d in (1, 7, 2, 6, 3, 5, 4):
        zo = (z - d) % NZ
        take(got.at[zo], ("out z", d))
        total = total + place(marks_got[zo][0:1], got[zo])
    seqh[c] = total.astype(BF16)
    put(seqh.at[c], seqh.at[c], sibling, "half", "half")

    def project(h):
        w = awc[pl.ds(pl.multiple_of(h * HALF, 128), HALF), :]
        return jnp.concatenate([
            jnp.dot(seqh[h, pl.ds(pl.multiple_of(c * 128, 128), 128), :], w, preferred_element_type=F32),
            jnp.dot(seqh[h, pl.ds(pl.multiple_of((1 - c) * 128, 128), 128), :], w, preferred_element_type=F32),
        ], axis=0)

    part = project(c)
    take(seqh.at[1 - c], "half")
    proj = (part + project(1 - c)).astype(BF16)
    kv[z] = proj[:, 256:640]

    in_seg = (z % 4, 3 - z % 4)

    def low_sent(i, s):
        return None if s < 3 else (i == 3) | (i == 0)

    def low_got(i, s):
        return None if s < 3 else (i == 0) | (i == 1)

    def rest_sent(i, s):
        return (i >= s) & (i <= 2)

    def rest_got(i, s):
        return i >= s + 1

    def origin(way, s):
        return (z - s) % NZ if way == 0 else (z + s) % NZ

    def piece_of(way, part, s, k):
        return kv.at[origin(way, s), pl.ds(k * 64 + (0 if part == "low" else 128), 64)]

    def pass_on(way, part, s, k):
        when = low_sent(in_seg[way], s) if part == "low" else rest_sent(in_seg[way], s)
        block = piece_of(way, part, s, k)
        kind = (way, "low") if part == "low" and s < 3 else (way, part, s)
        put(block, block, (right, left)[way], kind, (way, part, s, k), when)

    def take_piece(way, part, s, k):
        when = low_got(in_seg[way], s) if part == "low" else rest_got(in_seg[way], s)
        take(piece_of(way, part, s + 1, k), (way, part, s, k), when)

    def to_pair(zo, group, when=None):
        for rows, cols in ((0, slice(0, 256)), (64, slice(256, 384))):
            put(kv.at[zo, rows : rows + 64, cols], c2.at[zo, :, cols], x_pair, group, group, when)

    for part in ("low", "rest"):
        for k in (0, 1):
            for way in (0, 1):
                pass_on(way, part, 0, k)
    to_pair(z, "pair 0")

    lane256 = iota((256, 128), 1)
    q01 = proj[:, 0:128].astype(F32)
    q2 = proj[:, 128:256].astype(F32)
    qm[0] = jnp.where(lane256 < 64, q01, 0.0).astype(BF16)
    qm[1] = jnp.where(lane256 < 64, 0.0, q01).astype(BF16)
    qm[2] = jnp.where(lane256 < 64, q2, 0.0).astype(BF16)

    rr, cc = iota((256, 256), 0), iota((256, 256), 1)
    both = jnp.where((rr < 128) & (cc < 128), 2.0, 1.0)
    mask_s[0] = both + jnp.where((rr < 64) & (cc < 64), 1.0, 0.0)
    mask_s[1] = both + jnp.where((rr >= 64) & (rr < 128) & (cc >= 64) & (cc < 128), 1.0, 0.0)

    key_cols = (0, 0, 256)
    value_cols = (128, 128, 256)

    def update(h, lo, rows, keys, values, mult, fresh=False):
        at = pl.ds(lo, rows)
        s = nt_dot(qm[h, at, :], keys)
        top = jnp.max(s, axis=1, keepdims=True)
        if fresh:
            m_new = top
        else:
            m_old = m_s[h, at, :]
            m_new = jnp.maximum(m_old, top)
            keep = jnp.exp2((m_old - m_new) * EXP2_SCALE)
        p = jnp.exp2((s - m_new) * EXP2_SCALE)
        if mult is not None:
            p = p * mult
        total_p = jnp.sum(p, axis=1, keepdims=True)
        pv = jnp.dot(p.astype(BF16), values, preferred_element_type=F32)
        m_s[h, at, :] = m_new
        if fresh:
            l_s[h, at, :] = total_p
            acc_s[h, at, :] = pv
        else:
            l_s[h, at, :] = l_s[h, at, :] * keep + total_p
            acc_s[h, at, :] = acc_s[h, at, :] * keep + pv

    def full_block(zo, fresh=False):
        for h in range(3):
            update(
                h, 0, 256, kv[zo, :, key_cols[h] : key_cols[h] + 128],
                kv[zo, :, value_cols[h] : value_cols[h] + 128], mask_s[h // 2], fresh,
            )

    def part_block(zo):
        for h in range(3):
            update(
                h, 0, 128, kv[zo, 0:128, key_cols[h] : key_cols[h] + 128],
                kv[zo, 0:128, value_cols[h] : value_cols[h] + 128],
                mask_s[h // 2, 0:128, 0:128] - 1.0,
            )

    def pair_block(group, offsets):
        take(c2.at[0 : len(offsets)], group)
        blocks = [c2[z_of[e]] for e in offsets]
        block = jnp.concatenate(blocks, axis=0)
        for h in range(3):
            update(
                h, 64 * (h // 2), 64, block[:, key_cols[h] : key_cols[h] + 128],
                block[:, value_cols[h] : value_cols[h] + 128], None,
            )

    full_block(z, fresh=True)
    for s in range(4):
        for k in (0, 1):
            for way in (0, 1):
                take_piece(way, "low", s, k)
                if s < 3:
                    pass_on(way, "low", s + 1, k)
        for way in (0, 1):
            to_pair(origin(way, s + 1), "pair 0" if s < 2 else "pair 1", low_got(in_seg[way], s))
        if s < 3:
            for k in (0, 1):
                for way in (0, 1):
                    take_piece(way, "rest", s, k)
                    if s < 2:
                        pass_on(way, "rest", s + 1, k)
        if s == 3:
            pair_block("pair 0", (0, 7, 1, 6, 2))
        for way in (0, 1):
            zo = origin(way, s + 1)
            got_low = low_got(in_seg[way], s)
            if s < 3:
                full = rest_got(in_seg[way], s)
                pl.when(full)(lambda: full_block(zo))
                part = jnp.logical_not(full)
                pl.when(part if got_low is None else part & got_low)(lambda: part_block(zo))
            else:
                pl.when(got_low)(lambda: part_block(zo))
    pair_block("pair 1", (3, 5, 4))

    heads = [acc_s[h] / l_s[h] for h in range(3)]
    done = jnp.concatenate(
        [jnp.where(lane256 < 64, heads[0], heads[1]), heads[2]], axis=1
    ).astype(BF16)
    p_row, n_col = iota((128, 256), 0), iota((128, 256), 1)

    def arranged(oc):
        res = p_row % 4
        source = jnp.where(res % 2 == c, 0, 128) + (res // 2) * 64 + oc * 32 + p_row // 4
        hot = (n_col == source).astype(F32).astype(BF16)
        rows = jnp.dot(hot, done, preferred_element_type=F32)
        a, b = rows[:, 0:128], rows[:, 128:256]
        a_rolled, b_rolled = roll64(a), roll64(b)
        return jnp.concatenate([
            jnp.where(c == 0, a, a_rolled),
            jnp.where(c == 0, b_rolled, b),
            jnp.where(c == 0, a_rolled, a),
        ], axis=1)

    fin[0] = arranged(1 - c).astype(BF16)
    put(fin.at[0], fin.at[1], sibling, "fin", "fin")
    mine = arranged(c)
    take(fin.at[1], "fin")
    own_lane = (iota((128, HALF), 1) // 64) % 2 == c
    out_ref[...] = jnp.where(own_lane, mine, fin[1].astype(F32)).astype(BF16)

    for kind, ref in (
        ("z", wbuf.at[0, 0:3]), ("x", wbuf.at[0, 0:3]), ("cross", wbuf.at[0, 0, 0]), ("far", wbuf.at[0, 0:4]),
        ("bx", wbuf.at[0:3, 0:7, 0]), ("az", wbuf.at[0:3, 0:3, 0]), ("afar", wbuf.at[0:3, 0:4, 0]),
        ("pos", pos_sib), ("emb", emb_sib), ("mark x", marks_mid.at[0:3]), ("mark z", marks_got.at[0:7]),
        ("out x", xout), ("out z", got.at[0:7]), ("half", seqh.at[0]), ("fin", fin.at[0]),
        ("pair 0", c2.at[0:5]), ("pair 1", c2.at[0:3]),
    ):
        sent(ref, kind)
    for way in (0, 1):
        i = in_seg[way]
        sent(kv.at[0:3, 0:128], (way, "low"))
        sent(kv.at[0, 0:128], (way, "low", 3), low_sent(i, 3))
        for s in (0, 1, 2):
            sent(kv.at[0, 0:128], (way, "rest", s), rest_sent(i, s))
    assert len(names) <= N_SEMS, len(names)


def local(tile_embeddings, tile_position, input_weight, attention_weight):
    vmem = pl.BlockSpec(memory_space=pltpu.VMEM)
    anywhere = pl.BlockSpec(memory_space=pl.ANY)
    scratch = [
        pltpu.VMEM((1, SLOTS), jnp.int32),
        pltpu.VMEM((W_ROWS, 2 * HALF), BF16),
        pltpu.VMEM((SLOTS, E), BF16),
        pltpu.VMEM((SLOTS, E), BF16),
        pltpu.VMEM((1, SLOTS), jnp.int32),
        pltpu.VMEM((NX, NZ, 2, W_ROWS, HALF), BF16),
        pltpu.VMEM((D, 1152), BF16),
        pltpu.VMEM((D, 640), BF16),
        pltpu.VMEM((NX, NZ, 128), F32),
        pltpu.VMEM((NX, NZ, 128), F32),
        pltpu.VMEM((NZ, 8, 128), F32),
        pltpu.VMEM((NZ, 8, 128), F32),
        pltpu.VMEM((NX, 256, 2 * SLOTS), BF16),
        pltpu.VMEM((2 * SLOTS, HALF), BF16),
        pltpu.VMEM((NX, NZ, 32, HALF), BF16),
        pltpu.VMEM((NZ, NX, 32, HALF), BF16),
        pltpu.VMEM((3, NZ, 32, HALF), BF16),
        pltpu.VMEM((NZ, 256, HALF), BF16),
        pltpu.VMEM((NZ, 64, HALF), BF16),
        pltpu.VMEM((3, 256, 128), BF16),
        pltpu.VMEM((3, 256, 1), F32),
        pltpu.VMEM((3, 256, 1), F32),
        pltpu.VMEM((3, 256, 128), F32),
        pltpu.VMEM((2, 256, 256), F32),
        pltpu.VMEM((2, 128, HALF), BF16),
        pltpu.VMEM((2, 256, HALF), BF16),
        pltpu.SemaphoreType.DMA((N_SEMS,)),
        pltpu.SemaphoreType.DMA((4,)),
    ]
    return pl.pallas_call(
        kernel,
        out_shape=jax.ShapeDtypeStruct((TOK_DEV, HALF), BF16),
        in_specs=[anywhere] * 4,
        out_specs=vmem,
        scratch_shapes=scratch,
        compiler_params=pltpu.CompilerParams(
            collective_id=0, has_side_effects=True, vmem_limit_bytes=60 * 1024 * 1024
        ),
    )(tile_embeddings, tile_position.reshape(1, SLOTS), input_weight, attention_weight)


def solution(mesh):
    in_specs = (P(("slide", "seq"), None), P(("slide", "seq")), P("seq", None), P())
    out_specs = P(("slide", "seq"), None)
    return jax.shard_map(local, mesh=mesh, in_specs=in_specs, out_specs=out_specs, check_vma=False)
```

```python
import math

import jax
import jax.numpy as jnp
from jax import lax
from jax.experimental import pallas as pl
from jax.experimental.pallas import tpu as pltpu
from jax.sharding import PartitionSpec as P

E = 1536
D = 768
HALF = 384
TOK_DEV = 128
SLOTS = 256
NX = 4
NZ = 8
W_ROWS = 24
EXP2_SCALE = math.log2(math.e) * 64.0 ** -0.5
MESH = pl.DeviceIdType.MESH
F32 = jnp.float32
BF16 = jnp.bfloat16


def iota(shape, dim):
    return lax.broadcasted_iota(jnp.int32, shape, dim)


def nt_dot(a, b):
    return lax.dot_general(a, b, (((1,), (1,)), ((), ())), preferred_element_type=F32)


def roll64(a):
    return jnp.concatenate([a[:, 64:], a[:, :64]], axis=1)


N_SEMS = 112


def kernel(
    emb_in, pos_in, w_in, aw_in, out_ref,
    pos_ref, w_ref,
    emb_own, emb_sib, pos_sib, wbuf, awbuf, awc,
    marks, marks_mid, marks_z, marks_got,
    hot_s, seq, mid, got, xout, kv, c2, qm, m_s, l_s, acc_s, mask_s, low_mask_s, fin, seqh,
    sems, local_sems,
):
    me = lax.axis_index("seq")
    slide = lax.axis_index("slide")
    x, z, c = me // 16, (me % 16) // 2, me % 2

    def dev(xx, zz, cc):
        return (slide, xx * 16 + zz * 2 + cc)

    sibling = dev(x, z, 1 - c)
    x_of = [(x + d) % NX for d in range(NX)]
    z_of = [(z + d) % NZ for d in range(NZ)]
    right, left = dev(x, z_of[1], c), dev(x, z_of[7], c)
    x_pair = dev(x + 1 - 2 * (x % 2), z, c)

    names = {}

    def sem(name):
        return sems.at[names.setdefault(name, len(names))]

    def guarded(when, action):
        if when is None:
            action()
        else:
            pl.when(when)(action)

    def put(src, dst, target, sent_as, got_as, when=None):
        copy = pltpu.make_async_remote_copy(
            src_ref=src, dst_ref=dst, send_sem=sem(("sent", sent_as)), recv_sem=sem(got_as),
            device_id=target, device_id_type=MESH,
        )
        guarded(when, copy.start)

    def bytes_of(ref, name):
        return pltpu.make_async_remote_copy(
            src_ref=ref, dst_ref=ref, send_sem=sem(name), recv_sem=sem(name),
            device_id=sibling, device_id_type=MESH,
        )

    def take(ref, name, when=None):
        guarded(when, bytes_of(ref, name).wait_recv)
        return ref

    def sent(ref, name, when=None):
        guarded(when, bytes_of(ref, ("sent", name)).wait_send)

    w_load = pltpu.make_async_copy(w_in, w_ref, local_sems.at[0])
    pos_load = pltpu.make_async_copy(pos_in, pos_ref, local_sems.at[1])
    emb_load = pltpu.make_async_copy(emb_in, emb_own, local_sems.at[2])
    aw_load = pltpu.make_async_copy(aw_in, awbuf, local_sems.at[3])
    for load in (w_load, pos_load, emb_load, aw_load):
        load.start()

    barrier = pltpu.get_barrier_semaphore()
    partners = [sibling] + [dev(x_of[d], z, c) for d in (1, 2, 3)] + [dev(x, z_of[d], c) for d in range(1, 8)]
    partners += [dev(x_of[d], z, 1 - c) for d in (1, 2, 3)] + [dev(x, z_of[d], 1 - c) for d in (1, 4, 7)]
    for partner in partners:
        pl.semaphore_signal(barrier, inc=1, device_id=partner, device_id_type=MESH)
    pl.semaphore_wait(barrier, len(partners))

    w_load.wait()

    def w_half(h):
        return w_ref.at[:, pl.ds(pl.multiple_of(h * HALF, 128), HALF)]

    own_slot = wbuf.at[x, z, c]

    def w_give(kind, d, target_x, target_z):
        for half in (c, 1 - c):
            put(w_half(half), own_slot, dev(target_x, target_z, half), kind, (kind, d))

    for d in (4, 1, 7):
        w_give("z", d, x, z_of[d])
    for d in (1, 3, 2):
        w_give("x", d, x_of[d], z)
    put(w_half(1 - c), own_slot, sibling, "cross", "cross")
    pos_load.wait()
    put(pos_ref, pos_sib, sibling, "pos", "pos")
    emb_load.wait()
    put(emb_own, emb_sib, sibling, "emb", "emb")
    wbuf[x, z, c] = w_ref[:, pl.ds(pl.multiple_of(c * HALF, 128), HALF)]

    onward = {1: ((7, 2),), 7: ((1, 6),), 4: ((1, 3), (7, 5))}

    def w_pass_z(kind, slot, e, name):
        for to, seen in onward[e]:
            put(slot, slot, dev(x, z_of[to], c), kind, name(seen))

    def w_along_x(e):
        piece = wbuf.at[x, z_of[e], 1]
        for d in (1, 3, 2):
            put(piece, piece, dev(x_of[d], z, c), "bx", ("bx", d))

    def w_from_z(e):
        slot = take(wbuf.at[x, z_of[e]], ("z", 8 - e))
        w_pass_z("far", slot, e, lambda seen: ("far", seen))
        w_along_x(e)

    take(pos_sib, "pos")
    pos = jnp.concatenate([pos_ref[...], pos_sib[...]], axis=1)
    slots = 2 * SLOTS
    lane_t = iota((1, slots), 1)
    owner = pos >> 7
    chip = pos >> 8
    owner_hot = iota((64, slots), 0) == owner
    upper = (iota((slots, slots), 0) < iota((slots, slots), 1)) & (
        (iota((slots, slots), 0) // SLOTS) == (iota((slots, slots), 1) // SLOTS)
    )
    before = jnp.dot(
        owner_hot.astype(F32).astype(BF16), upper.astype(F32).astype(BF16), preferred_element_type=F32
    )
    rank = jnp.sum(jnp.where(owner_hot, before, 0.0), axis=0, keepdims=True)
    source_core = jnp.where(lane_t < SLOTS, c, 1 - c)
    target_row = jnp.where(pos >= 0, (owner * 16 + source_core * 8).astype(F32) + rank, -1.0)
    in_chip = jnp.where(pos >= 0, ((owner % 2) * 16 + source_core * 8).astype(F32) + rank, -1.0)
    chip_hot = (iota((32, slots), 0) == chip).astype(F32).astype(BF16)
    value = ((pos & 255) + 1).astype(F32)
    kind = iota((128, slots), 0)
    row_kind = (kind // 64 * 16 + kind % 16).astype(F32)
    marked = jnp.where(row_kind == in_chip, value, 0.0).astype(BF16)
    marks[...] = nt_dot(chip_hot, marked).reshape(NX, 8, 128)

    for d in (1, 3, 2):
        put(marks.at[x_of[d]], marks_mid.at[x], dev(x_of[d], z, c), "mark x", "mark x")

    for d in range(NX):
        rows = iota((256, slots), 0) + x_of[d] * 256
        hot_s[d] = (rows.astype(F32) == target_row).astype(F32).astype(BF16)

    w_from_z(1)
    w_from_z(7)
    for d in (1, 3, 2):
        xo = (x - d) % NX
        take(wbuf.at[xo, z], ("x", d))
        piece = wbuf.at[xo, z, 0]
        for to in (4, 1, 7):
            put(piece, piece, dev(x, z_of[to], c), "az", ("az", to, d))
    w_from_z(4)

    for e in (2, 6, 3, 5):
        take(wbuf.at[x, z_of[e]], ("far", e))
        w_along_x(e)
    for d in (1, 3, 2):
        xo = (x - d) % NX
        for e in (1, 7, 4):
            piece = take(wbuf.at[xo, z_of[e], 0], ("az", 8 - e, d))
            w_pass_z("afar", piece, e, lambda seen: ("afar", seen))

    take(marks_mid.at[0:3], "mark x")
    lane_group = iota((8, 128), 1) % 64 // 16
    merged = jnp.where(lane_group == x, marks[x], 0.0)
    for d in (1, 3, 2):
        xo = (x - d) % NX
        merged = merged + jnp.where(lane_group == xo, marks_mid[xo], 0.0)
    for zz in range(NZ):
        marks_z[zz] = jnp.broadcast_to(merged[zz : zz + 1], (8, 128))
    for d in range(1, NZ):
        put(marks_z.at[z_of[d]], marks_got.at[z], dev(x, z_of[d], c), "mark z", "mark z")

    take(wbuf.at[x, z, 1 - c], "cross")
    for d in (1, 3, 2):
        take(wbuf.at[(x - d) % NX, 0:7, 1], ("bx", d))
    for e in (2, 6, 3, 5):
        take(wbuf.at[0:3, z_of[e], 0], ("afar", e))

    weight = wbuf[...].reshape(E, HALF)
    seq[0:SLOTS] = jnp.dot(emb_own[...], weight, preferred_element_type=F32).astype(BF16)
    take(emb_sib, "emb")
    seq[SLOTS:] = jnp.dot(emb_sib[...], weight, preferred_element_type=F32).astype(BF16)

    def rows_for(d):
        rows = jnp.dot(hot_s[d], seq[...], preferred_element_type=F32)
        return rows.astype(BF16).reshape(NZ, 2, 16, HALF)

    def send_x(d, oc):
        put(xout.at[d - 1, :, oc], mid.at[x, :, oc], dev(x_of[d], z, c), "out x", ("out x", d, oc))

    def send_z(d, oc):
        xo = (x - d) % NX
        for e in (4, 3, 5, 2, 6, 1, 7):
            put(mid.at[xo, z_of[e], oc], got.at[z, oc, xo], dev(x, z_of[e], c), "out z", ("out z", e, oc))

    for d in (1, 3):
        xout[d - 1] = rows_for(d)
        send_x(d, 0)
    mid[x] = rows_for(0)
    send_z(0, 0)
    xout[1] = rows_for(2)
    send_x(2, 0)
    for d in (1, 3, 2):
        send_x(d, 1)
    send_z(0, 1)
    for oc in (0, 1):
        for d in (1, 3, 2):
            take(mid.at[(x - d) % NX, :, oc], ("out x", d, oc))
            send_z(d, oc)

    aw_load.wait()
    lane = iota((D, 128), 1)

    def pair(group_a, group_b):
        a = awbuf[:, group_a * 128 : group_a * 128 + 128].astype(F32)
        b = awbuf[:, group_b * 128 : group_b * 128 + 128].astype(F32)
        even = jnp.where(lane < 64, a, roll64(b))
        odd = jnp.where(lane < 64, roll64(a), b)
        return jnp.where(c == 0, even, odd).astype(BF16)

    awc[:, 0:128] = pair(0, 2)
    awc[:, 128:256] = pair(1, 1)
    awc[:, 256:384] = pair(3, 5)
    awc[:, 384:512] = pair(6, 8)
    awc[:, 512:640] = pair(4, 7)

    row = iota((128, 64), 0)
    group = row // 32
    first_wanted = row % 32 * 4 + group % 2 * 2 + group // 2 + 1

    def place(oc, zo_marks, rows):
        wanted = (first_wanted + oc * 128).astype(F32)
        hot = (zo_marks[:, oc * 64 : oc * 64 + 64] == wanted).astype(F32).astype(BF16)
        return jnp.dot(hot, rows.reshape(64, HALF), preferred_element_type=F32)

    def project(h, oc):
        w = awc[pl.ds(pl.multiple_of(h * HALF, 128), HALF), :]
        rows = jnp.concatenate([
            seqh[h, oc, pl.ds(pl.multiple_of(c * 64, 64), 64), :],
            seqh[h, oc, pl.ds(pl.multiple_of((1 - c) * 64, 64), 64), :],
        ], axis=0)
        return jnp.dot(rows, w, preferred_element_type=F32)

    take(marks_got.at[0:7], "mark z")

    def projections_of(oc):
        total = place(oc, marks_z[z][0:1], mid[:, z, oc])
        for d in (1, 7, 2, 6, 3, 5, 4):
            zo = (z - d) % NZ
            take(got.at[zo, oc], ("out z", d, oc))
            total = total + place(oc, marks_got[zo][0:1], got[zo, oc])
        seqh[c, oc] = total.astype(BF16)
        put(seqh.at[c, oc], seqh.at[c, oc], sibling, "half", ("half", oc))
        part = project(c, oc)
        take(seqh.at[1 - c, oc], ("half", oc))
        proj = (part + project(1 - c, oc)).astype(BF16)
        kv[z, oc] = proj[:, 256:640]
        return proj

    in_seg = (z % 4, 3 - z % 4)

    def low_sent(i, s):
        return None if s < 3 else (i == 3) | (i == 0)

    def low_got(i, s):
        return None if s < 3 else (i == 0) | (i == 1)

    def rest_sent(i, s):
        return (i >= s) & (i <= 2)

    def rest_got(i, s):
        return i >= s + 1

    def origin(way, s):
        return (z - s) % NZ if way == 0 else (z + s) % NZ

    def piece_of(way, part, s, k):
        return kv.at[origin(way, s), k, pl.ds(0 if part == "low" else 64, 64)]

    def pass_on(way, part, s, k):
        when = low_sent(in_seg[way], s) if part == "low" else rest_sent(in_seg[way], s)
        block = piece_of(way, part, s, k)
        kind = (way, "low") if part == "low" and s < 3 else (way, part, s)
        put(block, block, (right, left)[way], kind, (way, part, s, k), when)

    def take_piece(way, part, s, k):
        when = low_got(in_seg[way], s) if part == "low" else rest_got(in_seg[way], s)
        take(piece_of(way, part, s + 1, k), (way, part, s, k), when)

    def to_pair(zo, oc, group, when=None):
        for rows, cols in ((0, slice(0, 256)), (32, slice(256, 384))):
            put(
                kv.at[zo, oc, rows : rows + 32, cols], c2.at[zo, oc * 32 : oc * 32 + 32, cols], x_pair,
                group, group, when,
            )

    projected = []
    for oc in (0, 1):
        projected.append(projections_of(oc).astype(F32))
        for part in ("low", "rest"):
            for way in (0, 1):
                pass_on(way, part, 0, oc)
        to_pair(z, oc, "pair 0")

    lane256 = iota((256, 128), 1)
    query = jnp.concatenate(
        [projected[oc][g * 32 : g * 32 + 32, 0:256] for g in range(4) for oc in (0, 1)], axis=0
    )
    q01 = query[:, 0:128]
    q2 = query[:, 128:256]
    qm[0] = jnp.where(lane256 < 64, q01, 0.0).astype(BF16)
    qm[1] = jnp.where(lane256 < 64, 0.0, q01).astype(BF16)
    qm[2] = jnp.where(lane256 < 64, q2, 0.0).astype(BF16)

    rr, cc = iota((128, 256), 0), iota((128, 256), 1) % 128
    low_col = jnp.where(cc < 64, 2.0, 1.0)
    mask_s[0] = low_col + jnp.where((rr < 64) & (cc < 32), 1.0, 0.0)
    mask_s[1] = low_col + jnp.where((rr >= 64) & (cc >= 32) & (cc < 64), 1.0, 0.0)
    low_mask = [jnp.concatenate([mask_s[n, :, 0:64], mask_s[n, :, 128:192]], axis=1) - 1.0 for n in (0, 1)]
    for n in (0, 1):
        low_mask_s[n] = low_mask[n]

    key_cols = (0, 0, 256)
    value_cols = (128, 128, 256)

    def update(h, lo, rows, keys, values, mult, fresh=False):
        at = pl.ds(lo, rows)
        s = nt_dot(qm[h, at, :], keys)
        top = jnp.max(s, axis=1, keepdims=True)
        if fresh:
            m_new = top
        else:
            m_old = m_s[h, at, :]
            m_new = jnp.maximum(m_old, top)
            keep = jnp.exp2((m_old - m_new) * EXP2_SCALE)
        p = jnp.exp2((s - m_new) * EXP2_SCALE)
        if rows == 256:
            p = jnp.concatenate([p[0:128] * mult, p[128:]], axis=0)
        elif mult is not None:
            p = p * mult
        total_p = jnp.sum(p, axis=1, keepdims=True)
        pv = jnp.dot(p.astype(BF16), values, preferred_element_type=F32)
        m_s[h, at, :] = m_new
        if fresh:
            l_s[h, at, :] = total_p
            acc_s[h, at, :] = pv
        else:
            l_s[h, at, :] = l_s[h, at, :] * keep + total_p
            acc_s[h, at, :] = acc_s[h, at, :] * keep + pv

    def full_head(zo, h, fresh=False):
        update(
            h, 0, 256, kv[zo, :, :, key_cols[h] : key_cols[h] + 128].reshape(256, 128),
            kv[zo, :, :, value_cols[h] : value_cols[h] + 128].reshape(256, 128), mask_s[h // 2], fresh,
        )

    def part_head(zo, h):
        update(
            h, 0, 128, kv[zo, :, 0:64, key_cols[h] : key_cols[h] + 128].reshape(128, 128),
            kv[zo, :, 0:64, value_cols[h] : value_cols[h] + 128].reshape(128, 128), low_mask_s[h // 2],
        )

    def pair_head(offsets, h):
        at = lambda e, col: c2[z_of[e], :, col : col + 128]
        update(
            h, 64 * (h // 2), 64, jnp.concatenate([at(e, key_cols[h]) for e in offsets], axis=0),
            jnp.concatenate([at(e, value_cols[h]) for e in offsets], axis=0), None,
        )

    tasks = []

    def run(count):
        for _ in range(min(count, len(tasks))):
            tasks.pop(0)()

    def arrived_head(way, s, h):
        zo = origin(way, s + 1)
        if s == 3:
            pl.when(low_got(in_seg[way], s))(lambda: part_head(zo, h))
        else:
            full = rest_got(in_seg[way], s)
            pl.when(full)(lambda: full_head(zo, h))
            pl.when(jnp.logical_not(full))(lambda: part_head(zo, h))

    def later(action, *args):
        tasks.append(lambda: action(*args))

    for h in range(3):
        full_head(z, h, fresh=True)
    for s in range(4):
        for k in (0, 1):
            run(1)
            for way in (0, 1):
                take_piece(way, "low", s, k)
                if s < 3:
                    pass_on(way, "low", s + 1, k)
                to_pair(
                    origin(way, s + 1), k, "pair 0" if s < 2 else "pair 1",
                    None if s < 3 else low_got(in_seg[way], s),
                )
        if s < 3:
            for k in (0, 1):
                run(2)
                for way in (0, 1):
                    take_piece(way, "rest", s, k)
                    if s < 2:
                        pass_on(way, "rest", s + 1, k)
        for way in (0, 1):
            for h in range(3):
                later(arrived_head, way, s, h)
        if s == 2:
            run(3)
            take(c2.at[0:5], "pair 0")
            for h in range(3):
                later(pair_head, (0, 7, 1, 6, 2), h)
    run(len(tasks))
    take(c2.at[0:3], "pair 1")
    for h in range(3):
        pair_head((3, 5, 4), h)

    heads = [acc_s[h] / l_s[h] for h in range(3)]
    done = jnp.concatenate(
        [jnp.where(lane256 < 64, heads[0], heads[1]), heads[2]], axis=1
    ).astype(BF16)
    p_row, n_col = iota((128, 256), 0), iota((128, 256), 1)

    def arranged(oc):
        res = p_row % 4
        source = jnp.where(res % 2 == c, 0, 128) + (res // 2) * 64 + oc * 32 + p_row // 4
        hot = (n_col == source).astype(F32).astype(BF16)
        rows = jnp.dot(hot, done, preferred_element_type=F32)
        a, b = rows[:, 0:128], rows[:, 128:256]
        a_rolled, b_rolled = roll64(a), roll64(b)
        return jnp.concatenate([
            jnp.where(c == 0, a, a_rolled),
            jnp.where(c == 0, b_rolled, b),
            jnp.where(c == 0, a_rolled, a),
        ], axis=1)

    fin[0] = arranged(1 - c).astype(BF16)
    put(fin.at[0], fin.at[1], sibling, "fin", "fin")
    mine = arranged(c)
    take(fin.at[1], "fin")
    own_lane = (iota((128, HALF), 1) // 64) % 2 == c
    out_ref[...] = jnp.where(own_lane, mine, fin[1].astype(F32)).astype(BF16)

    for kind, ref in (
        ("z", wbuf.at[0, 0:3]), ("x", wbuf.at[0, 0:3]), ("cross", wbuf.at[0, 0, 0]), ("far", wbuf.at[0, 0:4]),
        ("bx", wbuf.at[0:3, 0:7, 0]), ("az", wbuf.at[0:3, 0:3, 0]), ("afar", wbuf.at[0:3, 0:4, 0]),
        ("pos", pos_sib), ("emb", emb_sib), ("mark x", marks_mid.at[0:3]), ("mark z", marks_got.at[0:7]),
        ("out x", xout), ("out z", got.at[0:7]), ("half", seqh.at[0]), ("fin", fin.at[0]),
        ("pair 0", c2.at[0:5]), ("pair 1", c2.at[0:3]),
    ):
        sent(ref, kind)
    for way in (0, 1):
        i = in_seg[way]
        sent(kv.at[0:3, :, 0:64], (way, "low"))
        sent(kv.at[0, :, 0:64], (way, "low", 3), low_sent(i, 3))
        for s in (0, 1, 2):
            sent(kv.at[0, :, 0:64], (way, "rest", s), rest_sent(i, s))
    assert len(names) <= N_SEMS, len(names)


def local(tile_embeddings, tile_position, input_weight, attention_weight):
    vmem = pl.BlockSpec(memory_space=pltpu.VMEM)
    anywhere = pl.BlockSpec(memory_space=pl.ANY)
    scratch = [
        pltpu.VMEM((1, SLOTS), jnp.int32),
        pltpu.VMEM((W_ROWS, 2 * HALF), BF16),
        pltpu.VMEM((SLOTS, E), BF16),
        pltpu.VMEM((SLOTS, E), BF16),
        pltpu.VMEM((1, SLOTS), jnp.int32),
        pltpu.VMEM((NX, NZ, 2, W_ROWS, HALF), BF16),
        pltpu.VMEM((D, 1152), BF16),
        pltpu.VMEM((D, 640), BF16),
        pltpu.VMEM((NX, NZ, 128), F32),
        pltpu.VMEM((NX, NZ, 128), F32),
        pltpu.VMEM((NZ, 8, 128), F32),
        pltpu.VMEM((NZ, 8, 128), F32),
        pltpu.VMEM((NX, 256, 2 * SLOTS), BF16),
        pltpu.VMEM((2 * SLOTS, HALF), BF16),
        pltpu.VMEM((NX, NZ, 2, 16, HALF), BF16),
        pltpu.VMEM((NZ, 2, NX, 16, HALF), BF16),
        pltpu.VMEM((3, NZ, 2, 16, HALF), BF16),
        pltpu.VMEM((NZ, 2, 128, HALF), BF16),
        pltpu.VMEM((NZ, 64, HALF), BF16),
        pltpu.VMEM((3, 256, 128), BF16),
        pltpu.VMEM((3, 256, 1), F32),
        pltpu.VMEM((3, 256, 1), F32),
        pltpu.VMEM((3, 256, 128), F32),
        pltpu.VMEM((2, 128, 256), F32),
        pltpu.VMEM((2, 128, 128), F32),
        pltpu.VMEM((2, 128, HALF), BF16),
        pltpu.VMEM((2, 2, 128, HALF), BF16),
        pltpu.SemaphoreType.DMA((N_SEMS,)),
        pltpu.SemaphoreType.DMA((4,)),
    ]
    return pl.pallas_call(
        kernel,
        out_shape=jax.ShapeDtypeStruct((TOK_DEV, HALF), BF16),
        in_specs=[anywhere] * 4,
        out_specs=vmem,
        scratch_shapes=scratch,
        compiler_params=pltpu.CompilerParams(
            collective_id=0, has_side_effects=True, vmem_limit_bytes=60 * 1024 * 1024
        ),
    )(tile_embeddings, tile_position.reshape(1, SLOTS), input_weight, attention_weight)


def solution(mesh):
    in_specs = (P(("slide", "seq"), None), P(("slide", "seq")), P("seq", None), P())
    out_specs = P(("slide", "seq"), None)
    return jax.shard_map(local, mesh=mesh, in_specs=in_specs, out_specs=out_specs, check_vma=False)
```

```python
import math

import jax
import jax.numpy as jnp
from jax import lax
from jax.experimental import pallas as pl
from jax.experimental.pallas import tpu as pltpu
from jax.sharding import PartitionSpec as P

E = 1536
D = 768
HALF = 384
TOK_DEV = 128
SLOTS = 256
NX = 4
NZ = 8
W_ROWS = 24
EXP2_SCALE = math.log2(math.e) * 64.0 ** -0.5
MESH = pl.DeviceIdType.MESH
F32 = jnp.float32
BF16 = jnp.bfloat16


def iota(shape, dim):
    return lax.broadcasted_iota(jnp.int32, shape, dim)


def nt_dot(a, b):
    return lax.dot_general(a, b, (((1,), (1,)), ((), ())), preferred_element_type=F32)


def roll64(a):
    return jnp.concatenate([a[:, 64:], a[:, :64]], axis=1)


N_SEMS = 113


def kernel(
    emb_in, pos_in, w_in, aw_in, out_ref,
    pos_ref, w_ref,
    emb_own, emb_sib, pos_sib, wbuf, awbuf, awc,
    marks, marks_mid, marks_z, marks_got,
    hot_s, seq, mid, got, xout, kv, c2, qm, m_s, l_s, acc_s, mask_s, low_mask_s, fin, seqh,
    sems, local_sems,
):
    me = lax.axis_index("seq")
    slide = lax.axis_index("slide")
    x, z, c = me // 16, (me % 16) // 2, me % 2

    def dev(xx, zz, cc):
        return (slide, xx * 16 + zz * 2 + cc)

    sibling = dev(x, z, 1 - c)
    x_of = [(x + d) % NX for d in range(NX)]
    z_of = [(z + d) % NZ for d in range(NZ)]
    right, left = dev(x, z_of[1], c), dev(x, z_of[7], c)
    x_pair = dev(x + 1 - 2 * (x % 2), z, c)

    names = {}

    def sem(name):
        return sems.at[names.setdefault(name, len(names))]

    def guarded(when, action):
        if when is None:
            action()
        else:
            pl.when(when)(action)

    def put(src, dst, target, sent_as, got_as, when=None):
        copy = pltpu.make_async_remote_copy(
            src_ref=src, dst_ref=dst, send_sem=sem(("sent", sent_as)), recv_sem=sem(got_as),
            device_id=target, device_id_type=MESH,
        )
        guarded(when, copy.start)

    def bytes_of(ref, name):
        return pltpu.make_async_remote_copy(
            src_ref=ref, dst_ref=ref, send_sem=sem(name), recv_sem=sem(name),
            device_id=sibling, device_id_type=MESH,
        )

    def take(ref, name, when=None):
        guarded(when, bytes_of(ref, name).wait_recv)
        return ref

    def sent(ref, name, when=None):
        guarded(when, bytes_of(ref, ("sent", name)).wait_send)

    w_load = pltpu.make_async_copy(w_in, w_ref, local_sems.at[0])
    pos_load = pltpu.make_async_copy(pos_in, pos_ref, local_sems.at[1])
    emb_load = pltpu.make_async_copy(emb_in, emb_own, local_sems.at[2])
    aw_load = pltpu.make_async_copy(aw_in, awbuf, local_sems.at[3])
    for load in (w_load, pos_load, emb_load, aw_load):
        load.start()

    barrier = pltpu.get_barrier_semaphore()
    partners = [sibling] + [dev(x_of[d], z, c) for d in (1, 2, 3)] + [dev(x, z_of[d], c) for d in range(1, 8)]
    partners += [dev(x_of[d], z, 1 - c) for d in (1, 2, 3)] + [dev(x, z_of[d], 1 - c) for d in (1, 2, 6, 7)]
    for partner in partners:
        pl.semaphore_signal(barrier, inc=1, device_id=partner, device_id_type=MESH)
    pl.semaphore_wait(barrier, len(partners))

    w_load.wait()

    def w_half(h):
        return w_ref.at[:, pl.ds(pl.multiple_of(h * HALF, 128), HALF)]

    own_slot = wbuf.at[x, z, c]

    def w_give(kind, d, target_x, target_z):
        for half in (c, 1 - c):
            put(w_half(half), own_slot, dev(target_x, target_z, half), kind, (kind, d))

    for d in (2, 6, 1, 7):
        w_give("z", d, x, z_of[d])
    for d in (1, 3, 2):
        w_give("x", d, x_of[d], z)
    put(w_half(1 - c), own_slot, sibling, "cross", "cross")
    pos_load.wait()
    put(pos_ref, pos_sib, sibling, "pos", "pos")
    emb_load.wait()
    put(emb_own, emb_sib, sibling, "emb", "emb")
    wbuf[x, z, c] = w_ref[:, pl.ds(pl.multiple_of(c * HALF, 128), HALF)]

    def w_to(kind, piece, to, name):
        put(piece, piece, dev(x, z_of[to], c), kind, name)

    def w_along_x(e):
        piece = wbuf.at[x, z_of[e], 1]
        for d in (1, 3, 2):
            put(piece, piece, dev(x_of[d], z, c), "bx", ("bx", d))

    take(pos_sib, "pos")
    pos = jnp.concatenate([pos_ref[...], pos_sib[...]], axis=1)
    slots = 2 * SLOTS
    lane_t = iota((1, slots), 1)
    owner = pos >> 7
    chip = pos >> 8
    owner_hot = iota((64, slots), 0) == owner
    upper = (iota((slots, slots), 0) < iota((slots, slots), 1)) & (
        (iota((slots, slots), 0) // SLOTS) == (iota((slots, slots), 1) // SLOTS)
    )
    before = jnp.dot(
        owner_hot.astype(F32).astype(BF16), upper.astype(F32).astype(BF16), preferred_element_type=F32
    )
    rank = jnp.sum(jnp.where(owner_hot, before, 0.0), axis=0, keepdims=True)
    source_core = jnp.where(lane_t < SLOTS, c, 1 - c)
    target_row = jnp.where(pos >= 0, (owner * 16 + source_core * 8).astype(F32) + rank, -1.0)
    in_chip = jnp.where(pos >= 0, ((owner % 2) * 16 + source_core * 8).astype(F32) + rank, -1.0)
    chip_hot = (iota((32, slots), 0) == chip).astype(F32).astype(BF16)
    value = ((pos & 255) + 1).astype(F32)
    kind = iota((128, slots), 0)
    row_kind = (kind // 64 * 16 + kind % 16).astype(F32)
    marked = jnp.where(row_kind == in_chip, value, 0.0).astype(BF16)
    marks[...] = nt_dot(chip_hot, marked).reshape(NX, 8, 128)

    for d in (1, 3, 2):
        put(marks.at[x_of[d]], marks_mid.at[x], dev(x_of[d], z, c), "mark x", "mark x")

    for d in range(NX):
        rows = iota((256, slots), 0) + x_of[d] * 256
        hot_s[d] = (rows.astype(F32) == target_row).astype(F32).astype(BF16)

    def w_from_x(d):
        take(wbuf.at[(x - d) % NX, z], ("x", d))
        piece = wbuf.at[(x - d) % NX, z, 0]
        for to in (2, 6, 1, 7):
            w_to("az", piece, to, ("az", to, d))

    w_from_x(1)
    w_from_x(3)
    for e, core, to, seen in ((2, 0, 7, 3), (6, 1, 1, 5)):
        block = take(wbuf.at[x, z_of[e]], ("z", 8 - e))
        w_to("far", block, to, ("far", seen))
        w_to("far", wbuf.at[x, z_of[e], core], 8 - e, ("far", 4))
    w_from_x(2)
    for e in (1, 7):
        take(wbuf.at[x, z_of[e]], ("z", 8 - e))
    for e in (2, 6, 1, 7):
        w_along_x(e)

    for d in (1, 3, 2):
        xo = (x - d) % NX
        for e, to, seen in ((2, 7, 3), (6, 1, 5)):
            piece = take(wbuf.at[xo, z_of[e], 0], ("az", 8 - e, d))
            w_to("afar", piece, to, ("afar", seen))
            if (e == 2) == (d != 3):
                w_to("afar", piece, 8 - e, ("afar", 4))
        if d == 3:
            for e in (3, 5, 4):
                take(wbuf.at[x, z_of[e]], ("far", e))
                w_along_x(e)
    for d in (1, 3, 2):
        for e in (1, 7):
            take(wbuf.at[(x - d) % NX, z_of[e], 0], ("az", 8 - e, d))

    take(marks_mid.at[0:3], "mark x")
    lane_group = iota((8, 128), 1) % 64 // 16
    merged = jnp.where(lane_group == x, marks[x], 0.0)
    for d in (1, 3, 2):
        xo = (x - d) % NX
        merged = merged + jnp.where(lane_group == xo, marks_mid[xo], 0.0)
    for zz in range(NZ):
        marks_z[zz] = jnp.broadcast_to(merged[zz : zz + 1], (8, 128))
    for d in range(1, NZ):
        put(marks_z.at[z_of[d]], marks_got.at[z], dev(x, z_of[d], c), "mark z", "mark z")

    take(wbuf.at[x, z, 1 - c], "cross")
    for d in (1, 3, 2):
        take(wbuf.at[(x - d) % NX, 0:7, 1], ("bx", d))
    for e in (3, 5, 4):
        take(wbuf.at[0:3, z_of[e], 0], ("afar", e))

    weight = wbuf[...].reshape(E, HALF)
    seq[0:SLOTS] = jnp.dot(emb_own[...], weight, preferred_element_type=F32).astype(BF16)
    take(emb_sib, "emb")
    seq[SLOTS:] = jnp.dot(emb_sib[...], weight, preferred_element_type=F32).astype(BF16)

    def rows_for(d):
        rows = jnp.dot(hot_s[d], seq[...], preferred_element_type=F32)
        return rows.astype(BF16).reshape(NZ, 2, 16, HALF)

    def send_x(d, oc):
        put(xout.at[d - 1, :, oc], mid.at[x, :, oc], dev(x_of[d], z, c), "out x", ("out x", d, oc))

    def send_z(d, oc):
        xo = (x - d) % NX
        for e in (4, 3, 5, 2, 6, 1, 7):
            put(mid.at[xo, z_of[e], oc], got.at[z, oc, xo], dev(x, z_of[e], c), "out z", ("out z", e, oc))

    for d in (1, 3):
        xout[d - 1] = rows_for(d)
        send_x(d, 0)
    mid[x] = rows_for(0)
    send_z(0, 0)
    xout[1] = rows_for(2)
    send_x(2, 0)
    for d in (1, 3, 2):
        send_x(d, 1)
    send_z(0, 1)
    for oc in (0, 1):
        for d in (1, 3, 2):
            take(mid.at[(x - d) % NX, :, oc], ("out x", d, oc))
            send_z(d, oc)

    aw_load.wait()
    lane = iota((D, 128), 1)

    def pair(group_a, group_b):
        a = awbuf[:, group_a * 128 : group_a * 128 + 128].astype(F32)
        b = awbuf[:, group_b * 128 : group_b * 128 + 128].astype(F32)
        even = jnp.where(lane < 64, a, roll64(b))
        odd = jnp.where(lane < 64, roll64(a), b)
        return jnp.where(c == 0, even, odd).astype(BF16)

    awc[:, 0:128] = pair(0, 2)
    awc[:, 128:256] = pair(1, 1)
    awc[:, 256:384] = pair(3, 5)
    awc[:, 384:512] = pair(6, 8)
    awc[:, 512:640] = pair(4, 7)

    row = iota((128, 64), 0)
    group = row // 32
    first_wanted = row % 32 * 4 + group % 2 * 2 + group // 2 + 1

    def place(oc, zo_marks, rows):
        wanted = (first_wanted + oc * 128).astype(F32)
        hot = (zo_marks[:, oc * 64 : oc * 64 + 64] == wanted).astype(F32).astype(BF16)
        return jnp.dot(hot, rows.reshape(64, HALF), preferred_element_type=F32)

    def project(h, oc):
        w = awc[pl.ds(pl.multiple_of(h * HALF, 128), HALF), :]
        rows = jnp.concatenate([
            seqh[h, oc, pl.ds(pl.multiple_of(c * 64, 64), 64), :],
            seqh[h, oc, pl.ds(pl.multiple_of((1 - c) * 64, 64), 64), :],
        ], axis=0)
        return jnp.dot(rows, w, preferred_element_type=F32)

    take(marks_got.at[0:7], "mark z")

    def projections_of(oc):
        total = place(oc, marks_z[z][0:1], mid[:, z, oc])
        for d in (1, 7, 2, 6, 3, 5, 4):
            zo = (z - d) % NZ
            take(got.at[zo, oc], ("out z", d, oc))
            total = total + place(oc, marks_got[zo][0:1], got[zo, oc])
        seqh[c, oc] = total.astype(BF16)
        put(seqh.at[c, oc], seqh.at[c, oc], sibling, "half", ("half", oc))
        part = project(c, oc)
        take(seqh.at[1 - c, oc], ("half", oc))
        proj = (part + project(1 - c, oc)).astype(BF16)
        kv[z, oc] = proj[:, 256:640]
        return proj

    in_seg = (z % 4, 3 - z % 4)

    def low_sent(i, s):
        return None if s < 3 else (i == 3) | (i == 0)

    def low_got(i, s):
        return None if s < 3 else (i == 0) | (i == 1)

    def rest_sent(i, s):
        return (i >= s) & (i <= 2)

    def rest_got(i, s):
        return i >= s + 1

    def origin(way, s):
        return (z - s) % NZ if way == 0 else (z + s) % NZ

    def piece_of(way, part, s, k):
        return kv.at[origin(way, s), k, pl.ds(0 if part == "low" else 64, 64)]

    def pass_on(way, part, s, k):
        when = low_sent(in_seg[way], s) if part == "low" else rest_sent(in_seg[way], s)
        block = piece_of(way, part, s, k)
        kind = (way, "low") if part == "low" and s < 3 else (way, part, s)
        put(block, block, (right, left)[way], kind, (way, part, s, k), when)

    def take_piece(way, part, s, k):
        when = low_got(in_seg[way], s) if part == "low" else rest_got(in_seg[way], s)
        take(piece_of(way, part, s + 1, k), (way, part, s, k), when)

    def to_pair(zo, oc, group, when=None):
        for rows, cols in ((0, slice(0, 256)), (32, slice(256, 384))):
            put(
                kv.at[zo, oc, rows : rows + 32, cols], c2.at[zo, oc * 32 : oc * 32 + 32, cols], x_pair,
                group, group, when,
            )

    projected = []
    for oc in (0, 1):
        projected.append(projections_of(oc).astype(F32))
        for part in ("low", "rest"):
            for way in (0, 1):
                pass_on(way, part, 0, oc)
        to_pair(z, oc, "pair 0")

    lane256 = iota((256, 128), 1)
    query = jnp.concatenate(
        [projected[oc][g * 32 : g * 32 + 32, 0:256] for g in range(4) for oc in (0, 1)], axis=0
    )
    q01 = query[:, 0:128]
    q2 = query[:, 128:256]
    qm[0] = jnp.where(lane256 < 64, q01, 0.0).astype(BF16)
    qm[1] = jnp.where(lane256 < 64, 0.0, q01).astype(BF16)
    qm[2] = jnp.where(lane256 < 64, q2, 0.0).astype(BF16)

    rr, cc = iota((128, 256), 0), iota((128, 256), 1) % 128
    low_col = jnp.where(cc < 64, 2.0, 1.0)
    mask_s[0] = low_col + jnp.where((rr < 64) & (cc < 32), 1.0, 0.0)
    mask_s[1] = low_col + jnp.where((rr >= 64) & (cc >= 32) & (cc < 64), 1.0, 0.0)
    low_mask = [jnp.concatenate([mask_s[n, :, 0:64], mask_s[n, :, 128:192]], axis=1) - 1.0 for n in (0, 1)]
    for n in (0, 1):
        low_mask_s[n] = low_mask[n]

    key_cols = (0, 0, 256)
    value_cols = (128, 128, 256)

    def update(h, lo, rows, keys, values, mult, fresh=False):
        at = pl.ds(lo, rows)
        s = nt_dot(qm[h, at, :], keys)
        top = jnp.max(s, axis=1, keepdims=True)
        if fresh:
            m_new = top
        else:
            m_old = m_s[h, at, :]
            m_new = jnp.maximum(m_old, top)
            keep = jnp.exp2((m_old - m_new) * EXP2_SCALE)
        p = jnp.exp2((s - m_new) * EXP2_SCALE)
        if rows == 256:
            p = jnp.concatenate([p[0:128] * mult, p[128:]], axis=0)
        elif mult is not None:
            p = p * mult
        total_p = jnp.sum(p, axis=1, keepdims=True)
        pv = jnp.dot(p.astype(BF16), values, preferred_element_type=F32)
        m_s[h, at, :] = m_new
        if fresh:
            l_s[h, at, :] = total_p
            acc_s[h, at, :] = pv
        else:
            l_s[h, at, :] = l_s[h, at, :] * keep + total_p
            acc_s[h, at, :] = acc_s[h, at, :] * keep + pv

    def full_head(zo, h, fresh=False):
        update(
            h, 0, 256, kv[zo, :, :, key_cols[h] : key_cols[h] + 128].reshape(256, 128),
            kv[zo, :, :, value_cols[h] : value_cols[h] + 128].reshape(256, 128), mask_s[h // 2], fresh,
        )

    def part_head(zo, h):
        update(
            h, 0, 128, kv[zo, :, 0:64, key_cols[h] : key_cols[h] + 128].reshape(128, 128),
            kv[zo, :, 0:64, value_cols[h] : value_cols[h] + 128].reshape(128, 128), low_mask_s[h // 2],
        )

    def pair_head(offsets, h):
        at = lambda e, col: c2[z_of[e], :, col : col + 128]
        update(
            h, 64 * (h // 2), 64, jnp.concatenate([at(e, key_cols[h]) for e in offsets], axis=0),
            jnp.concatenate([at(e, value_cols[h]) for e in offsets], axis=0), None,
        )

    tasks = []

    def run(count):
        for _ in range(min(count, len(tasks))):
            tasks.pop(0)()

    def arrived_head(way, s, h):
        zo = origin(way, s + 1)
        if s == 3:
            pl.when(low_got(in_seg[way], s))(lambda: part_head(zo, h))
        else:
            full = rest_got(in_seg[way], s)
            pl.when(full)(lambda: full_head(zo, h))
            pl.when(jnp.logical_not(full))(lambda: part_head(zo, h))

    def later(action, *args):
        tasks.append(lambda: action(*args))

    for h in range(3):
        full_head(z, h, fresh=True)
    for s in range(4):
        for k in (0, 1):
            run(1)
            for way in (0, 1):
                take_piece(way, "low", s, k)
                if s < 3:
                    pass_on(way, "low", s + 1, k)
                to_pair(
                    origin(way, s + 1), k, "pair 0" if s < 2 else "pair 1",
                    None if s < 3 else low_got(in_seg[way], s),
                )
        if s < 3:
            for k in (0, 1):
                run(2)
                for way in (0, 1):
                    take_piece(way, "rest", s, k)
                    if s < 2:
                        pass_on(way, "rest", s + 1, k)
        for way in (0, 1):
            for h in range(3):
                later(arrived_head, way, s, h)
        if s == 2:
            run(3)
            take(c2.at[0:5], "pair 0")
            for h in range(3):
                later(pair_head, (0, 7, 1, 6, 2), h)
    run(len(tasks))
    take(c2.at[0:3], "pair 1")
    for h in range(3):
        pair_head((3, 5, 4), h)

    heads = [acc_s[h] / l_s[h] for h in range(3)]
    done = jnp.concatenate(
        [jnp.where(lane256 < 64, heads[0], heads[1]), heads[2]], axis=1
    ).astype(BF16)
    p_row, n_col = iota((128, 256), 0), iota((128, 256), 1)

    def arranged(oc):
        res = p_row % 4
        source = jnp.where(res % 2 == c, 0, 128) + (res // 2) * 64 + oc * 32 + p_row // 4
        hot = (n_col == source).astype(F32).astype(BF16)
        rows = jnp.dot(hot, done, preferred_element_type=F32)
        a, b = rows[:, 0:128], rows[:, 128:256]
        a_rolled, b_rolled = roll64(a), roll64(b)
        return jnp.concatenate([
            jnp.where(c == 0, a, a_rolled),
            jnp.where(c == 0, b_rolled, b),
            jnp.where(c == 0, a_rolled, a),
        ], axis=1)

    fin[0] = arranged(1 - c).astype(BF16)
    put(fin.at[0], fin.at[1], sibling, "fin", "fin")
    mine = arranged(c)
    take(fin.at[1], "fin")
    own_lane = (iota((128, HALF), 1) // 64) % 2 == c
    out_ref[...] = jnp.where(own_lane, mine, fin[1].astype(F32)).astype(BF16)

    for kind, ref in (
        ("z", wbuf.at[0, 0:4]), ("x", wbuf.at[0, 0:3]), ("cross", wbuf.at[0, 0, 0]), ("far", wbuf.at[0, 0:3]),
        ("bx", wbuf.at[0:3, 0:7, 0]), ("az", wbuf.at[0:3, 0:4, 0]), ("afar", wbuf.at[0:3, 0:3, 0]),
        ("pos", pos_sib), ("emb", emb_sib), ("mark x", marks_mid.at[0:3]), ("mark z", marks_got.at[0:7]),
        ("out x", xout), ("out z", got.at[0:7]), ("half", seqh.at[0]), ("fin", fin.at[0]),
        ("pair 0", c2.at[0:5]), ("pair 1", c2.at[0:3]),
    ):
        sent(ref, kind)
    for way in (0, 1):
        i = in_seg[way]
        sent(kv.at[0:3, :, 0:64], (way, "low"))
        sent(kv.at[0, :, 0:64], (way, "low", 3), low_sent(i, 3))
        for s in (0, 1, 2):
            sent(kv.at[0, :, 0:64], (way, "rest", s), rest_sent(i, s))
    assert len(names) <= N_SEMS, len(names)


def local(tile_embeddings, tile_position, input_weight, attention_weight):
    vmem = pl.BlockSpec(memory_space=pltpu.VMEM)
    anywhere = pl.BlockSpec(memory_space=pl.ANY)
    scratch = [
        pltpu.VMEM((1, SLOTS), jnp.int32),
        pltpu.VMEM((W_ROWS, 2 * HALF), BF16),
        pltpu.VMEM((SLOTS, E), BF16),
        pltpu.VMEM((SLOTS, E), BF16),
        pltpu.VMEM((1, SLOTS), jnp.int32),
        pltpu.VMEM((NX, NZ, 2, W_ROWS, HALF), BF16),
        pltpu.VMEM((D, 1152), BF16),
        pltpu.VMEM((D, 640), BF16),
        pltpu.VMEM((NX, NZ, 128), F32),
        pltpu.VMEM((NX, NZ, 128), F32),
        pltpu.VMEM((NZ, 8, 128), F32),
        pltpu.VMEM((NZ, 8, 128), F32),
        pltpu.VMEM((NX, 256, 2 * SLOTS), BF16),
        pltpu.VMEM((2 * SLOTS, HALF), BF16),
        pltpu.VMEM((NX, NZ, 2, 16, HALF), BF16),
        pltpu.VMEM((NZ, 2, NX, 16, HALF), BF16),
        pltpu.VMEM((3, NZ, 2, 16, HALF), BF16),
        pltpu.VMEM((NZ, 2, 128, HALF), BF16),
        pltpu.VMEM((NZ, 64, HALF), BF16),
        pltpu.VMEM((3, 256, 128), BF16),
        pltpu.VMEM((3, 256, 1), F32),
        pltpu.VMEM((3, 256, 1), F32),
        pltpu.VMEM((3, 256, 128), F32),
        pltpu.VMEM((2, 128, 256), F32),
        pltpu.VMEM((2, 128, 128), F32),
        pltpu.VMEM((2, 128, HALF), BF16),
        pltpu.VMEM((2, 2, 128, HALF), BF16),
        pltpu.SemaphoreType.DMA((N_SEMS,)),
        pltpu.SemaphoreType.DMA((4,)),
    ]
    return pl.pallas_call(
        kernel,
        out_shape=jax.ShapeDtypeStruct((TOK_DEV, HALF), BF16),
        in_specs=[anywhere] * 4,
        out_specs=vmem,
        scratch_shapes=scratch,
        compiler_params=pltpu.CompilerParams(
            collective_id=0, has_side_effects=True, vmem_limit_bytes=60 * 1024 * 1024
        ),
    )(tile_embeddings, tile_position.reshape(1, SLOTS), input_weight, attention_weight)


def solution(mesh):
    in_specs = (P(("slide", "seq"), None), P(("slide", "seq")), P("seq", None), P())
    out_specs = P(("slide", "seq"), None)
    return jax.shard_map(local, mesh=mesh, in_specs=in_specs, out_specs=out_specs, check_vma=False)
```

```python
import math

import jax
import jax.numpy as jnp
from jax import lax
from jax.experimental import pallas as pl
from jax.experimental.pallas import tpu as pltpu
from jax.sharding import PartitionSpec as P

E = 1536
D = 768
HALF = 384
TOK_DEV = 128
SLOTS = 256
NX = 4
NZ = 8
W_ROWS = 24
EXP2_SCALE = math.log2(math.e) * 64.0 ** -0.5
MESH = pl.DeviceIdType.MESH
F32 = jnp.float32
BF16 = jnp.bfloat16


def iota(shape, dim):
    return lax.broadcasted_iota(jnp.int32, shape, dim)


def nt_dot(a, b):
    return lax.dot_general(a, b, (((1,), (1,)), ((), ())), preferred_element_type=F32)


def roll64(a):
    return jnp.concatenate([a[:, 64:], a[:, :64]], axis=1)


N_SEMS = 113


def kernel(
    emb_in, pos_in, w_in, aw_in, out_ref,
    pos_ref, w_ref,
    emb_own, emb_sib, pos_sib, wbuf, awbuf, awc,
    marks, marks_mid, marks_z, marks_got,
    hot_s, seq, mid, got, xout, kv, c2, qm, m_s, l_s, acc_s, mask_s, low_mask_s, fin, seqh,
    sems, local_sems,
):
    me = lax.axis_index("seq")
    slide = lax.axis_index("slide")
    x, z, c = me // 16, (me % 16) // 2, me % 2

    def dev(xx, zz, cc):
        return (slide, xx * 16 + zz * 2 + cc)

    sibling = dev(x, z, 1 - c)
    x_of = [(x + d) % NX for d in range(NX)]
    z_of = [(z + d) % NZ for d in range(NZ)]
    right, left = dev(x, z_of[1], c), dev(x, z_of[7], c)
    x_pair = dev(x + 1 - 2 * (x % 2), z, c)

    names = {}

    def sem(name):
        return sems.at[names.setdefault(name, len(names))]

    def guarded(when, action):
        if when is None:
            action()
        else:
            pl.when(when)(action)

    def put(src, dst, target, sent_as, got_as, when=None):
        copy = pltpu.make_async_remote_copy(
            src_ref=src, dst_ref=dst, send_sem=sem(("sent", sent_as)), recv_sem=sem(got_as),
            device_id=target, device_id_type=MESH,
        )
        guarded(when, copy.start)

    def bytes_of(ref, name):
        return pltpu.make_async_remote_copy(
            src_ref=ref, dst_ref=ref, send_sem=sem(name), recv_sem=sem(name),
            device_id=sibling, device_id_type=MESH,
        )

    def take(ref, name, when=None):
        guarded(when, bytes_of(ref, name).wait_recv)
        return ref

    def sent(ref, name, when=None):
        guarded(when, bytes_of(ref, ("sent", name)).wait_send)

    w_load = pltpu.make_async_copy(w_in, w_ref, local_sems.at[0])
    pos_load = pltpu.make_async_copy(pos_in, pos_ref, local_sems.at[1])
    emb_load = pltpu.make_async_copy(emb_in, emb_own, local_sems.at[2])
    aw_load = pltpu.make_async_copy(aw_in, awbuf, local_sems.at[3])
    for load in (w_load, pos_load, emb_load, aw_load):
        load.start()

    barrier = pltpu.get_barrier_semaphore()
    partners = [sibling] + [dev(x_of[d], z, c) for d in (1, 2, 3)] + [dev(x, z_of[d], c) for d in (1, 2, 6, 7)]
    partners += [dev(x_of[d], z, 1 - c) for d in (1, 2, 3)] + [dev(x, z_of[d], 1 - c) for d in (1, 2, 6, 7)]
    for partner in partners:
        pl.semaphore_signal(barrier, inc=1, device_id=partner, device_id_type=MESH)
    pl.semaphore_wait(barrier, len(partners))

    w_load.wait()

    def w_half(h):
        return w_ref.at[:, pl.ds(pl.multiple_of(h * HALF, 128), HALF)]

    own_slot = wbuf.at[x, z, c]

    def w_give(kind, d, target_x, target_z):
        for half in (c, 1 - c):
            put(w_half(half), own_slot, dev(target_x, target_z, half), kind, (kind, d))

    for d in (2, 6, 1, 7):
        w_give("z", d, x, z_of[d])
    for d in (1, 3, 2):
        w_give("x", d, x_of[d], z)
    put(w_half(1 - c), own_slot, sibling, "cross", "cross")
    pos_load.wait()
    put(pos_ref, pos_sib, sibling, "pos", "pos")
    emb_load.wait()
    put(emb_own, emb_sib, sibling, "emb", "emb")
    wbuf[x, z, c] = w_ref[:, pl.ds(pl.multiple_of(c * HALF, 128), HALF)]

    def w_to(kind, piece, to, name):
        put(piece, piece, dev(x, z_of[to], c), kind, name)

    def w_along_x(e):
        piece = wbuf.at[x, z_of[e], 1]
        for d in (1, 3, 2):
            put(piece, piece, dev(x_of[d], z, c), "bx", ("bx", d))

    take(pos_sib, "pos")
    pos = jnp.concatenate([pos_ref[...], pos_sib[...]], axis=1)
    slots = 2 * SLOTS
    lane_t = iota((1, slots), 1)
    owner = pos >> 7
    chip = pos >> 8
    owner_hot = iota((64, slots), 0) == owner
    upper = (iota((slots, slots), 0) < iota((slots, slots), 1)) & (
        (iota((slots, slots), 0) // SLOTS) == (iota((slots, slots), 1) // SLOTS)
    )
    before = jnp.dot(
        owner_hot.astype(F32).astype(BF16), upper.astype(F32).astype(BF16), preferred_element_type=F32
    )
    rank = jnp.sum(jnp.where(owner_hot, before, 0.0), axis=0, keepdims=True)
    source_core = jnp.where(lane_t < SLOTS, c, 1 - c)
    target_row = jnp.where(pos >= 0, (owner * 16 + source_core * 8).astype(F32) + rank, -1.0)
    in_chip = jnp.where(pos >= 0, ((owner % 2) * 16 + source_core * 8).astype(F32) + rank, -1.0)
    chip_hot = (iota((32, slots), 0) == chip).astype(F32).astype(BF16)
    value = ((pos & 255) + 1).astype(F32)
    kind = iota((128, slots), 0)
    row_kind = (kind // 64 * 16 + kind % 16).astype(F32)
    marked = jnp.where(row_kind == in_chip, value, 0.0).astype(BF16)
    marks[...] = nt_dot(chip_hot, marked).reshape(NX, 8, 128)

    for d in (1, 3, 2):
        put(marks.at[x_of[d]], marks_mid.at[x], dev(x_of[d], z, c), "mark x", "mark x")

    for d in range(NX):
        rows = iota((256, slots), 0) + x_of[d] * 256
        hot_s[d] = (rows.astype(F32) == target_row).astype(F32).astype(BF16)

    def w_from_x(d):
        take(wbuf.at[(x - d) % NX, z], ("x", d))
        piece = wbuf.at[(x - d) % NX, z, 0]
        for to in (2, 6, 1, 7):
            w_to("az", piece, to, ("az", to, d))

    w_from_x(1)
    w_from_x(3)
    for e, core, to, seen in ((2, 0, 7, 3), (6, 1, 1, 5)):
        block = take(wbuf.at[x, z_of[e]], ("z", 8 - e))
        w_to("far", block, to, ("far", seen))
        w_to("far", wbuf.at[x, z_of[e], core], 8 - e, ("far", 4))
    w_from_x(2)
    for e in (1, 7):
        take(wbuf.at[x, z_of[e]], ("z", 8 - e))
    for e in (2, 6, 1, 7):
        w_along_x(e)

    for d in (1, 3, 2):
        xo = (x - d) % NX
        for e, to, seen in ((2, 7, 3), (6, 1, 5)):
            piece = take(wbuf.at[xo, z_of[e], 0], ("az", 8 - e, d))
            w_to("afar", piece, to, ("afar", seen))
            if (e == 2) == (d != 3):
                w_to("afar", piece, 8 - e, ("afar", 4))
        if d == 3:
            for e in (3, 5, 4):
                take(wbuf.at[x, z_of[e]], ("far", e))
                w_along_x(e)
    for d in (1, 3, 2):
        for e in (1, 7):
            take(wbuf.at[(x - d) % NX, z_of[e], 0], ("az", 8 - e, d))

    take(marks_mid.at[0:3], "mark x")
    lane_group = iota((8, 128), 1) % 64 // 16
    merged = jnp.where(lane_group == x, marks[x], 0.0)
    for d in (1, 3, 2):
        xo = (x - d) % NX
        merged = merged + jnp.where(lane_group == xo, marks_mid[xo], 0.0)
    for zz in range(NZ):
        marks_z[zz] = jnp.broadcast_to(merged[zz : zz + 1], (8, 128))
    for d in range(1, NZ):
        put(marks_z.at[z_of[d]], marks_got.at[z], dev(x, z_of[d], c), "mark z", "mark z")

    take(wbuf.at[x, z, 1 - c], "cross")
    for d in (1, 3, 2):
        take(wbuf.at[(x - d) % NX, 0:7, 1], ("bx", d))
    for e in (3, 5, 4):
        take(wbuf.at[0:3, z_of[e], 0], ("afar", e))

    weight = wbuf[...].reshape(E, HALF)
    seq[0:SLOTS] = jnp.dot(emb_own[...], weight, preferred_element_type=F32).astype(BF16)
    take(emb_sib, "emb")
    seq[SLOTS:] = jnp.dot(emb_sib[...], weight, preferred_element_type=F32).astype(BF16)

    def rows_for(d):
        rows = jnp.dot(hot_s[d], seq[...], preferred_element_type=F32)
        return rows.astype(BF16).reshape(NZ, 2, 16, HALF)

    def send_x(d, oc):
        put(xout.at[d - 1, :, oc], mid.at[x, :, oc], dev(x_of[d], z, c), "out x", ("out x", d, oc))

    def send_z(d, oc):
        xo = (x - d) % NX
        for e in (4, 3, 5, 2, 6, 1, 7):
            put(mid.at[xo, z_of[e], oc], got.at[z, oc, xo], dev(x, z_of[e], c), "out z", ("out z", e, oc))

    for d in (1, 3):
        xout[d - 1] = rows_for(d)
        send_x(d, 0)
    mid[x] = rows_for(0)
    send_z(0, 0)
    xout[1] = rows_for(2)
    send_x(2, 0)
    for d in (1, 3, 2):
        send_x(d, 1)
    send_z(0, 1)
    for oc in (0, 1):
        for d in (1, 3, 2):
            take(mid.at[(x - d) % NX, :, oc], ("out x", d, oc))
            send_z(d, oc)

    aw_load.wait()
    lane = iota((D, 128), 1)

    def pair(group_a, group_b):
        a = awbuf[:, group_a * 128 : group_a * 128 + 128].astype(F32)
        b = awbuf[:, group_b * 128 : group_b * 128 + 128].astype(F32)
        even = jnp.where(lane < 64, a, roll64(b))
        odd = jnp.where(lane < 64, roll64(a), b)
        return jnp.where(c == 0, even, odd).astype(BF16)

    awc[:, 0:128] = pair(0, 2)
    awc[:, 128:256] = pair(1, 1)
    awc[:, 256:384] = pair(3, 5)
    awc[:, 384:512] = pair(6, 8)
    awc[:, 512:640] = pair(4, 7)

    row = iota((128, 64), 0)
    group = row // 32
    first_wanted = row % 32 * 4 + group % 2 * 2 + group // 2 + 1

    def place(oc, zo_marks, rows):
        wanted = (first_wanted + oc * 128).astype(F32)
        hot = (zo_marks[:, oc * 64 : oc * 64 + 64] == wanted).astype(F32).astype(BF16)
        return jnp.dot(hot, rows.reshape(64, HALF), preferred_element_type=F32)

    def project(h, oc):
        w = awc[pl.ds(pl.multiple_of(h * HALF, 128), HALF), :]
        rows = jnp.concatenate([
            seqh[h, oc, pl.ds(pl.multiple_of(c * 64, 64), 64), :],
            seqh[h, oc, pl.ds(pl.multiple_of((1 - c) * 64, 64), 64), :],
        ], axis=0)
        return jnp.dot(rows, w, preferred_element_type=F32)

    take(marks_got.at[0:7], "mark z")

    def projections_of(oc):
        total = place(oc, marks_z[z][0:1], mid[:, z, oc])
        for d in (1, 7, 2, 6, 3, 5, 4):
            zo = (z - d) % NZ
            take(got.at[zo, oc], ("out z", d, oc))
            total = total + place(oc, marks_got[zo][0:1], got[zo, oc])
        seqh[c, oc] = total.astype(BF16)
        put(seqh.at[c, oc], seqh.at[c, oc], sibling, "half", ("half", oc))
        part = project(c, oc)
        take(seqh.at[1 - c, oc], ("half", oc))
        proj = (part + project(1 - c, oc)).astype(BF16)
        kv[z, oc] = proj[:, 256:640]
        return proj

    in_seg = (z % 4, 3 - z % 4)

    def low_sent(i, s):
        return None if s < 3 else (i == 3) | (i == 0)

    def low_got(i, s):
        return None if s < 3 else (i == 0) | (i == 1)

    def rest_sent(i, s):
        return (i >= s) & (i <= 2)

    def rest_got(i, s):
        return i >= s + 1

    def origin(way, s):
        return (z - s) % NZ if way == 0 else (z + s) % NZ

    def piece_of(way, part, s, k):
        return kv.at[origin(way, s), k, pl.ds(0 if part == "low" else 64, 64)]

    def pass_on(way, part, s, k):
        when = low_sent(in_seg[way], s) if part == "low" else rest_sent(in_seg[way], s)
        block = piece_of(way, part, s, k)
        kind = (way, "low") if part == "low" and s < 3 else (way, part, s)
        put(block, block, (right, left)[way], kind, (way, part, s, k), when)

    def take_piece(way, part, s, k):
        when = low_got(in_seg[way], s) if part == "low" else rest_got(in_seg[way], s)
        take(piece_of(way, part, s + 1, k), (way, part, s, k), when)

    def to_pair(zo, oc, group, when=None):
        for rows, cols in ((0, slice(0, 256)), (32, slice(256, 384))):
            put(
                kv.at[zo, oc, rows : rows + 32, cols], c2.at[zo, oc * 32 : oc * 32 + 32, cols], x_pair,
                group, group, when,
            )

    projected = []
    for oc in (0, 1):
        projected.append(projections_of(oc).astype(F32))
        for part in ("low", "rest"):
            for way in (0, 1):
                pass_on(way, part, 0, oc)
        to_pair(z, oc, "pair 0")

    lane256 = iota((256, 128), 1)
    query = jnp.concatenate(
        [projected[oc][g * 32 : g * 32 + 32, 0:256] for g in range(4) for oc in (0, 1)], axis=0
    )
    q01 = query[:, 0:128]
    q2 = query[:, 128:256]
    qm[0] = jnp.where(lane256 < 64, q01, 0.0).astype(BF16)
    qm[1] = jnp.where(lane256 < 64, 0.0, q01).astype(BF16)
    qm[2] = jnp.where(lane256 < 64, q2, 0.0).astype(BF16)

    rr, cc = iota((128, 256), 0), iota((128, 256), 1) % 128
    low_col = jnp.where(cc < 64, 2.0, 1.0)
    mask_s[0] = low_col + jnp.where((rr < 64) & (cc < 32), 1.0, 0.0)
    mask_s[1] = low_col + jnp.where((rr >= 64) & (cc >= 32) & (cc < 64), 1.0, 0.0)
    low_mask = [jnp.concatenate([mask_s[n, :, 0:64], mask_s[n, :, 128:192]], axis=1) - 1.0 for n in (0, 1)]
    for n in (0, 1):
        low_mask_s[n] = low_mask[n]

    key_cols = (0, 0, 256)
    value_cols = (128, 128, 256)

    def update(h, lo, rows, keys, values, mult, fresh=False):
        at = pl.ds(lo, rows)
        s = nt_dot(qm[h, at, :], keys)
        top = jnp.max(s, axis=1, keepdims=True)
        if fresh:
            m_new = top
        else:
            m_old = m_s[h, at, :]
            m_new = jnp.maximum(m_old, top)
            keep = jnp.exp2((m_old - m_new) * EXP2_SCALE)
        p = jnp.exp2((s - m_new) * EXP2_SCALE)
        if rows == 256:
            p = jnp.concatenate([p[0:128] * mult, p[128:]], axis=0)
        elif mult is not None:
            p = p * mult
        total_p = jnp.sum(p, axis=1, keepdims=True)
        pv = jnp.dot(p.astype(BF16), values, preferred_element_type=F32)
        m_s[h, at, :] = m_new
        if fresh:
            l_s[h, at, :] = total_p
            acc_s[h, at, :] = pv
        else:
            l_s[h, at, :] = l_s[h, at, :] * keep + total_p
            acc_s[h, at, :] = acc_s[h, at, :] * keep + pv

    def full_head(zo, h, fresh=False):
        update(
            h, 0, 256, kv[zo, :, :, key_cols[h] : key_cols[h] + 128].reshape(256, 128),
            kv[zo, :, :, value_cols[h] : value_cols[h] + 128].reshape(256, 128), mask_s[h // 2], fresh,
        )

    def part_head(zo, h):
        update(
            h, 0, 128, kv[zo, :, 0:64, key_cols[h] : key_cols[h] + 128].reshape(128, 128),
            kv[zo, :, 0:64, value_cols[h] : value_cols[h] + 128].reshape(128, 128), low_mask_s[h // 2],
        )

    def pair_head(offsets, h):
        at = lambda e, col: c2[z_of[e], :, col : col + 128]
        update(
            h, 64 * (h // 2), 64, jnp.concatenate([at(e, key_cols[h]) for e in offsets], axis=0),
            jnp.concatenate([at(e, value_cols[h]) for e in offsets], axis=0), None,
        )

    tasks = []

    def run(count):
        for _ in range(min(count, len(tasks))):
            tasks.pop(0)()

    def heads(head, *args):
        for h in range(3):
            head(*args, h)

    def arrived(way, s):
        zo = origin(way, s + 1)
        if s == 3:
            pl.when(low_got(in_seg[way], s))(lambda: heads(part_head, zo))
        else:
            full = rest_got(in_seg[way], s)
            pl.when(full)(lambda: heads(full_head, zo))
            pl.when(jnp.logical_not(full))(lambda: heads(part_head, zo))

    def later(action, *args):
        tasks.append(lambda: action(*args))

    later(lambda: [full_head(z, h, fresh=True) for h in range(3)])
    for s in range(4):
        for k in (0, 1):
            run(1 if s else k)
            for way in (0, 1):
                take_piece(way, "low", s, k)
                if s < 3:
                    pass_on(way, "low", s + 1, k)
                to_pair(
                    origin(way, s + 1), k, "pair 0" if s < 2 else "pair 1",
                    None if s < 3 else low_got(in_seg[way], s),
                )
        if s < 3:
            for k in (0, 1):
                run(1 - k)
                for way in (0, 1):
                    take_piece(way, "rest", s, k)
                    if s < 2:
                        pass_on(way, "rest", s + 1, k)
        for way in (0, 1):
            later(arrived, way, s)
        if s == 2:
            take(c2.at[0:5], "pair 0")
            later(heads, pair_head, (0, 7, 1, 6, 2))
    run(len(tasks))
    take(c2.at[0:3], "pair 1")
    heads(pair_head, (3, 5, 4))

    heads = [acc_s[h] / l_s[h] for h in range(3)]
    done = jnp.concatenate(
        [jnp.where(lane256 < 64, heads[0], heads[1]), heads[2]], axis=1
    ).astype(BF16)
    p_row, n_col = iota((128, 256), 0), iota((128, 256), 1)

    def arranged(oc):
        res = p_row % 4
        source = jnp.where(res % 2 == c, 0, 128) + (res // 2) * 64 + oc * 32 + p_row // 4
        hot = (n_col == source).astype(F32).astype(BF16)
        rows = jnp.dot(hot, done, preferred_element_type=F32)
        a, b = rows[:, 0:128], rows[:, 128:256]
        a_rolled, b_rolled = roll64(a), roll64(b)
        return jnp.concatenate([
            jnp.where(c == 0, a, a_rolled),
            jnp.where(c == 0, b_rolled, b),
            jnp.where(c == 0, a_rolled, a),
        ], axis=1)

    fin[0] = arranged(1 - c).astype(BF16)
    put(fin.at[0], fin.at[1], sibling, "fin", "fin")
    mine = arranged(c)
    take(fin.at[1], "fin")
    own_lane = (iota((128, HALF), 1) // 64) % 2 == c
    out_ref[...] = jnp.where(own_lane, mine, fin[1].astype(F32)).astype(BF16)

    for kind, ref in (
        ("z", wbuf.at[0, 0:4]), ("x", wbuf.at[0, 0:3]), ("cross", wbuf.at[0, 0, 0]), ("far", wbuf.at[0, 0:3]),
        ("bx", wbuf.at[0:3, 0:7, 0]), ("az", wbuf.at[0:3, 0:4, 0]), ("afar", wbuf.at[0:3, 0:3, 0]),
        ("pos", pos_sib), ("emb", emb_sib), ("mark x", marks_mid.at[0:3]), ("mark z", marks_got.at[0:7]),
        ("out x", xout), ("out z", got.at[0:7]), ("half", seqh.at[0]), ("fin", fin.at[0]),
        ("pair 0", c2.at[0:5]), ("pair 1", c2.at[0:3]),
    ):
        sent(ref, kind)
    for way in (0, 1):
        i = in_seg[way]
        sent(kv.at[0:3, :, 0:64], (way, "low"))
        sent(kv.at[0, :, 0:64], (way, "low", 3), low_sent(i, 3))
        for s in (0, 1, 2):
            sent(kv.at[0, :, 0:64], (way, "rest", s), rest_sent(i, s))
    assert len(names) <= N_SEMS, len(names)


def local(tile_embeddings, tile_position, input_weight, attention_weight):
    vmem = pl.BlockSpec(memory_space=pltpu.VMEM)
    anywhere = pl.BlockSpec(memory_space=pl.ANY)
    scratch = [
        pltpu.VMEM((1, SLOTS), jnp.int32),
        pltpu.VMEM((W_ROWS, 2 * HALF), BF16),
        pltpu.VMEM((SLOTS, E), BF16),
        pltpu.VMEM((SLOTS, E), BF16),
        pltpu.VMEM((1, SLOTS), jnp.int32),
        pltpu.VMEM((NX, NZ, 2, W_ROWS, HALF), BF16),
        pltpu.VMEM((D, 1152), BF16),
        pltpu.VMEM((D, 640), BF16),
        pltpu.VMEM((NX, NZ, 128), F32),
        pltpu.VMEM((NX, NZ, 128), F32),
        pltpu.VMEM((NZ, 8, 128), F32),
        pltpu.VMEM((NZ, 8, 128), F32),
        pltpu.VMEM((NX, 256, 2 * SLOTS), BF16),
        pltpu.VMEM((2 * SLOTS, HALF), BF16),
        pltpu.VMEM((NX, NZ, 2, 16, HALF), BF16),
        pltpu.VMEM((NZ, 2, NX, 16, HALF), BF16),
        pltpu.VMEM((3, NZ, 2, 16, HALF), BF16),
        pltpu.VMEM((NZ, 2, 128, HALF), BF16),
        pltpu.VMEM((NZ, 64, HALF), BF16),
        pltpu.VMEM((3, 256, 128), BF16),
        pltpu.VMEM((3, 256, 1), F32),
        pltpu.VMEM((3, 256, 1), F32),
        pltpu.VMEM((3, 256, 128), F32),
        pltpu.VMEM((2, 128, 256), F32),
        pltpu.VMEM((2, 128, 128), F32),
        pltpu.VMEM((2, 128, HALF), BF16),
        pltpu.VMEM((2, 2, 128, HALF), BF16),
        pltpu.SemaphoreType.DMA((N_SEMS,)),
        pltpu.SemaphoreType.DMA((4,)),
    ]
    return pl.pallas_call(
        kernel,
        out_shape=jax.ShapeDtypeStruct((TOK_DEV, HALF), BF16),
        in_specs=[anywhere] * 4,
        out_specs=vmem,
        scratch_shapes=scratch,
        compiler_params=pltpu.CompilerParams(
            collective_id=0, has_side_effects=True, vmem_limit_bytes=60 * 1024 * 1024
        ),
    )(tile_embeddings, tile_position.reshape(1, SLOTS), input_weight, attention_weight)


def solution(mesh):
    in_specs = (P(("slide", "seq"), None), P(("slide", "seq")), P("seq", None), P())
    out_specs = P(("slide", "seq"), None)
    return jax.shard_map(local, mesh=mesh, in_specs=in_specs, out_specs=out_specs, check_vma=False)
```

```python
import math

import jax
import jax.numpy as jnp
from jax import lax
from jax.experimental import pallas as pl
from jax.experimental.pallas import tpu as pltpu
from jax.sharding import PartitionSpec as P

E = 1536
D = 768
HALF = 384
TOK_DEV = 128
SLOTS = 256
NX = 4
NZ = 8
W_ROWS = 24
EXP2_SCALE = math.log2(math.e) * 64.0 ** -0.5
MESH = pl.DeviceIdType.MESH
F32 = jnp.float32
BF16 = jnp.bfloat16


def iota(shape, dim):
    return lax.broadcasted_iota(jnp.int32, shape, dim)


def nt_dot(a, b):
    return lax.dot_general(a, b, (((1,), (1,)), ((), ())), preferred_element_type=F32)


def roll64(a):
    return jnp.concatenate([a[:, 64:], a[:, :64]], axis=1)


N_SEMS = 113


def kernel(
    emb_in, pos_in, w_in, aw_in, out_ref,
    pos_ref, w_ref,
    emb_own, emb_sib, pos_sib, wbuf, awbuf, awc,
    marks, marks_mid, marks_z, marks_got,
    hot_s, seq, mid, got, xout, kv, c2, qm, m_s, l_s, acc_s, mask_s, low_mask_s, place_s, back_s, fin, seqh,
    sems, local_sems,
):
    me = lax.axis_index("seq")
    slide = lax.axis_index("slide")
    x, z, c = me // 16, (me % 16) // 2, me % 2

    def dev(xx, zz, cc):
        return (slide, xx * 16 + zz * 2 + cc)

    sibling = dev(x, z, 1 - c)
    x_of = [(x + d) % NX for d in range(NX)]
    z_of = [(z + d) % NZ for d in range(NZ)]
    right, left = dev(x, z_of[1], c), dev(x, z_of[7], c)
    x_pair = dev(x + 1 - 2 * (x % 2), z, c)

    names = {}

    def sem(name):
        return sems.at[names.setdefault(name, len(names))]

    def guarded(when, action):
        if when is None:
            action()
        else:
            pl.when(when)(action)

    def put(src, dst, target, sent_as, got_as, when=None):
        copy = pltpu.make_async_remote_copy(
            src_ref=src, dst_ref=dst, send_sem=sem(("sent", sent_as)), recv_sem=sem(got_as),
            device_id=target, device_id_type=MESH,
        )
        guarded(when, copy.start)

    def bytes_of(ref, name):
        return pltpu.make_async_remote_copy(
            src_ref=ref, dst_ref=ref, send_sem=sem(name), recv_sem=sem(name),
            device_id=sibling, device_id_type=MESH,
        )

    def take(ref, name, when=None):
        guarded(when, bytes_of(ref, name).wait_recv)
        return ref

    def sent(ref, name, when=None):
        guarded(when, bytes_of(ref, ("sent", name)).wait_send)

    w_load = pltpu.make_async_copy(w_in, w_ref, local_sems.at[0])
    pos_load = pltpu.make_async_copy(pos_in, pos_ref, local_sems.at[1])
    emb_load = pltpu.make_async_copy(emb_in, emb_own, local_sems.at[2])
    aw_load = pltpu.make_async_copy(aw_in, awbuf, local_sems.at[3])
    for load in (w_load, pos_load, emb_load, aw_load):
        load.start()

    barrier = pltpu.get_barrier_semaphore()
    partners = [sibling] + [dev(x_of[d], z, c) for d in (1, 2, 3)] + [dev(x, z_of[d], c) for d in (1, 2, 6, 7)]
    partners += [dev(x_of[d], z, 1 - c) for d in (1, 2, 3)] + [dev(x, z_of[d], 1 - c) for d in (1, 2, 6, 7)]
    for partner in partners:
        pl.semaphore_signal(barrier, inc=1, device_id=partner, device_id_type=MESH)
    pl.semaphore_wait(barrier, len(partners))

    w_load.wait()

    def w_half(h):
        return w_ref.at[:, pl.ds(pl.multiple_of(h * HALF, 128), HALF)]

    own_slot = wbuf.at[x, z, c]

    def w_give(kind, d, target_x, target_z):
        for half in (c, 1 - c):
            put(w_half(half), own_slot, dev(target_x, target_z, half), kind, (kind, d))

    for d in (2, 6, 1, 7):
        w_give("z", d, x, z_of[d])
    for d in (1, 3, 2):
        w_give("x", d, x_of[d], z)
    put(w_half(1 - c), own_slot, sibling, "cross", "cross")
    pos_load.wait()
    put(pos_ref, pos_sib, sibling, "pos", "pos")
    emb_load.wait()
    put(emb_own, emb_sib, sibling, "emb", "emb")
    wbuf[x, z, c] = w_ref[:, pl.ds(pl.multiple_of(c * HALF, 128), HALF)]

    def w_to(kind, piece, to, name):
        put(piece, piece, dev(x, z_of[to], c), kind, name)

    def w_along_x(e):
        piece = wbuf.at[x, z_of[e], 1]
        for d in (1, 3, 2):
            put(piece, piece, dev(x_of[d], z, c), "bx", ("bx", d))

    take(pos_sib, "pos")
    pos = jnp.concatenate([pos_ref[...], pos_sib[...]], axis=1)
    slots = 2 * SLOTS
    lane_t = iota((1, slots), 1)
    owner = pos >> 7
    chip = pos >> 8
    owner_hot = iota((64, slots), 0) == owner
    upper = (iota((slots, slots), 0) < iota((slots, slots), 1)) & (
        (iota((slots, slots), 0) // SLOTS) == (iota((slots, slots), 1) // SLOTS)
    )
    before = jnp.dot(
        owner_hot.astype(F32).astype(BF16), upper.astype(F32).astype(BF16), preferred_element_type=F32
    )
    rank = jnp.sum(jnp.where(owner_hot, before, 0.0), axis=0, keepdims=True)
    source_core = jnp.where(lane_t < SLOTS, c, 1 - c)
    target_row = jnp.where(pos >= 0, (owner * 16 + source_core * 8).astype(F32) + rank, -1.0)
    in_chip = jnp.where(pos >= 0, ((owner % 2) * 16 + source_core * 8).astype(F32) + rank, -1.0)
    chip_hot = (iota((32, slots), 0) == chip).astype(F32).astype(BF16)
    value = ((pos & 255) + 1).astype(F32)
    kind = iota((128, slots), 0)
    row_kind = (kind // 64 * 16 + kind % 16).astype(F32)
    marked = jnp.where(row_kind == in_chip, value, 0.0).astype(BF16)
    marks[...] = nt_dot(chip_hot, marked).reshape(NX, 8, 128)

    for d in (1, 3, 2):
        put(marks.at[x_of[d]], marks_mid.at[x], dev(x_of[d], z, c), "mark x", "mark x")

    for d in range(NX):
        rows = iota((256, slots), 0) + x_of[d] * 256
        hot_s[d] = (rows.astype(F32) == target_row).astype(F32).astype(BF16)

    def w_from_x(d):
        take(wbuf.at[(x - d) % NX, z], ("x", d))
        piece = wbuf.at[(x - d) % NX, z, 0]
        for to in (2, 6, 1, 7):
            w_to("az", piece, to, ("az", to, d))

    w_from_x(1)
    w_from_x(3)
    for e, core, to, seen in ((2, 0, 7, 3), (6, 1, 1, 5)):
        block = take(wbuf.at[x, z_of[e]], ("z", 8 - e))
        w_to("far", block, to, ("far", seen))
        w_to("far", wbuf.at[x, z_of[e], core], 8 - e, ("far", 4))
    w_from_x(2)
    for e in (1, 7):
        take(wbuf.at[x, z_of[e]], ("z", 8 - e))
    for e in (2, 6, 1, 7):
        w_along_x(e)

    for d in (1, 3, 2):
        xo = (x - d) % NX
        for e, to, seen in ((2, 7, 3), (6, 1, 5)):
            piece = take(wbuf.at[xo, z_of[e], 0], ("az", 8 - e, d))
            w_to("afar", piece, to, ("afar", seen))
            if (e == 2) == (d != 3):
                w_to("afar", piece, 8 - e, ("afar", 4))
        if d == 3:
            for e in (3, 5, 4):
                take(wbuf.at[x, z_of[e]], ("far", e))
                w_along_x(e)
    for d in (1, 3, 2):
        for e in (1, 7):
            take(wbuf.at[(x - d) % NX, z_of[e], 0], ("az", 8 - e, d))

    take(marks_mid.at[0:3], "mark x")
    lane_group = iota((8, 128), 1) % 64 // 16
    merged = jnp.where(lane_group == x, marks[x], 0.0)
    for d in (1, 3, 2):
        xo = (x - d) % NX
        merged = merged + jnp.where(lane_group == xo, marks_mid[xo], 0.0)
    for zz in range(NZ):
        marks_z[zz] = jnp.broadcast_to(merged[zz : zz + 1], (8, 128))
    for d in range(1, NZ):
        put(marks_z.at[z_of[d]], marks_got.at[z], dev(x, z_of[d], c), "mark z", "mark z")

    take(wbuf.at[x, z, 1 - c], "cross")
    for d in (1, 3, 2):
        take(wbuf.at[(x - d) % NX, 0:7, 1], ("bx", d))
    for e in (3, 5, 4):
        take(wbuf.at[0:3, z_of[e], 0], ("afar", e))

    weight = wbuf[...].reshape(E, HALF)
    seq[0:SLOTS] = jnp.dot(emb_own[...], weight, preferred_element_type=F32).astype(BF16)
    take(emb_sib, "emb")
    seq[SLOTS:] = jnp.dot(emb_sib[...], weight, preferred_element_type=F32).astype(BF16)

    def rows_for(d):
        rows = jnp.dot(hot_s[d], seq[...], preferred_element_type=F32)
        return rows.astype(BF16).reshape(NZ, 2, 16, HALF)

    def send_x(d, oc):
        put(xout.at[d - 1, :, oc], mid.at[x, :, oc], dev(x_of[d], z, c), "out x", ("out x", d, oc))

    def send_z(d, oc):
        xo = (x - d) % NX
        for e in (4, 3, 5, 2, 6, 1, 7):
            put(mid.at[xo, z_of[e], oc], got.at[z, oc, xo], dev(x, z_of[e], c), "out z", ("out z", e, oc))

    for d in (1, 3):
        xout[d - 1] = rows_for(d)
        send_x(d, 0)
    mid[x] = rows_for(0)
    send_z(0, 0)
    xout[1] = rows_for(2)
    send_x(2, 0)
    for d in (1, 3, 2):
        send_x(d, 1)
    send_z(0, 1)
    for oc in (0, 1):
        for d in (1, 3, 2):
            take(mid.at[(x - d) % NX, :, oc], ("out x", d, oc))
            send_z(d, oc)

    aw_load.wait()
    lane = iota((D, 128), 1)

    def pair(group_a, group_b):
        a = awbuf[:, group_a * 128 : group_a * 128 + 128].astype(F32)
        b = awbuf[:, group_b * 128 : group_b * 128 + 128].astype(F32)
        even = jnp.where(lane < 64, a, roll64(b))
        odd = jnp.where(lane < 64, roll64(a), b)
        return jnp.where(c == 0, even, odd).astype(BF16)

    awc[:, 0:128] = pair(0, 2)
    awc[:, 128:256] = pair(1, 1)
    awc[:, 256:384] = pair(3, 5)
    awc[:, 384:512] = pair(6, 8)
    awc[:, 512:640] = pair(4, 7)

    row = iota((128, 64), 0)
    group = row // 32
    first_wanted = row % 32 * 4 + group % 2 * 2 + group // 2 + 1

    def place(oc, zo_marks):
        wanted = (first_wanted + oc * 128).astype(F32)
        return (zo_marks[:, oc * 64 : oc * 64 + 64] == wanted).astype(F32)

    def project(h, oc):
        w = awc[pl.ds(pl.multiple_of(h * HALF, 128), HALF), :]
        rows = jnp.concatenate([
            seqh[h, oc, pl.ds(pl.multiple_of(c * 64, 64), 64), :],
            seqh[h, oc, pl.ds(pl.multiple_of((1 - c) * 64, 64), 64), :],
        ], axis=0)
        return jnp.dot(rows, w, preferred_element_type=F32)

    take(marks_got.at[0:7], "mark z")
    all_marks = [marks_z[z][0:1]] + [marks_got[(z - d) % NZ][0:1] for d in (1, 7, 2, 6, 3, 5, 4)]
    for oc in (0, 1):
        place_s[oc] = jnp.concatenate([place(oc, marked) for marked in all_marks], axis=1).astype(BF16)

    p_row, n_col = iota((128, 256), 0), iota((128, 256), 1)
    for n, oc in enumerate((1 - c, c)):
        res = p_row % 4
        source = jnp.where(res % 2 == c, 0, 128) + (res // 2) * 64 + oc * 32 + p_row // 4
        back_s[n] = (n_col == source).astype(F32).astype(BF16)

    def projections_of(oc):
        blocks = [mid[:, z, oc].reshape(64, HALF)]
        for d in (1, 7, 2, 6, 3, 5, 4):
            zo = (z - d) % NZ
            take(got.at[zo, oc], ("out z", d, oc))
            blocks.append(got[zo, oc].reshape(64, HALF))
        total = jnp.dot(place_s[oc], jnp.concatenate(blocks, axis=0), preferred_element_type=F32)
        seqh[c, oc] = total.astype(BF16)
        put(seqh.at[c, oc], seqh.at[c, oc], sibling, "half", ("half", oc))
        part = project(c, oc)
        take(seqh.at[1 - c, oc], ("half", oc))
        proj = (part + project(1 - c, oc)).astype(BF16)
        kv[z, oc] = proj[:, 256:640]
        return proj

    in_seg = (z % 4, 3 - z % 4)

    def low_sent(i, s):
        return None if s < 3 else (i == 3) | (i == 0)

    def low_got(i, s):
        return None if s < 3 else (i == 0) | (i == 1)

    def rest_sent(i, s):
        return (i >= s) & (i <= 2)

    def rest_got(i, s):
        return i >= s + 1

    def origin(way, s):
        return (z - s) % NZ if way == 0 else (z + s) % NZ

    def piece_of(way, part, s, k):
        return kv.at[origin(way, s), k, pl.ds(0 if part == "low" else 64, 64)]

    def pass_on(way, part, s, k):
        when = low_sent(in_seg[way], s) if part == "low" else rest_sent(in_seg[way], s)
        block = piece_of(way, part, s, k)
        kind = (way, "low") if part == "low" and s < 3 else (way, part, s)
        put(block, block, (right, left)[way], kind, (way, part, s, k), when)

    def take_piece(way, part, s, k):
        when = low_got(in_seg[way], s) if part == "low" else rest_got(in_seg[way], s)
        take(piece_of(way, part, s + 1, k), (way, part, s, k), when)

    def to_pair(zo, oc, group, when=None):
        for rows, cols in ((0, slice(0, 256)), (32, slice(256, 384))):
            put(
                kv.at[zo, oc, rows : rows + 32, cols], c2.at[zo, oc * 32 : oc * 32 + 32, cols], x_pair,
                group, group, when,
            )

    projected = []
    for oc in (0, 1):
        projected.append(projections_of(oc).astype(F32))
        for part in ("low", "rest"):
            for way in (0, 1):
                pass_on(way, part, 0, oc)
        to_pair(z, oc, "pair 0")

    lane256 = iota((256, 128), 1)
    query = jnp.concatenate(
        [projected[oc][g * 32 : g * 32 + 32, 0:256] for g in range(4) for oc in (0, 1)], axis=0
    )
    q01 = query[:, 0:128]
    q2 = query[:, 128:256]
    qm[0] = jnp.where(lane256 < 64, q01, 0.0).astype(BF16)
    qm[1] = jnp.where(lane256 < 64, 0.0, q01).astype(BF16)
    qm[2] = jnp.where(lane256 < 64, q2, 0.0).astype(BF16)

    rr, cc = iota((128, 256), 0), iota((128, 256), 1) % 128
    low_col = jnp.where(cc < 64, 2.0, 1.0)
    mask_s[0] = low_col + jnp.where((rr < 64) & (cc < 32), 1.0, 0.0)
    mask_s[1] = low_col + jnp.where((rr >= 64) & (cc >= 32) & (cc < 64), 1.0, 0.0)
    low_mask = [jnp.concatenate([mask_s[n, :, 0:64], mask_s[n, :, 128:192]], axis=1) - 1.0 for n in (0, 1)]
    for n in (0, 1):
        low_mask_s[n] = low_mask[n]

    key_cols = (0, 0, 256)
    value_cols = (128, 128, 256)

    def update(h, lo, rows, keys, values, mult, fresh=False):
        at = pl.ds(lo, rows)
        s = nt_dot(qm[h, at, :], keys)
        top = jnp.max(s, axis=1, keepdims=True)
        if fresh:
            m_new = top
        else:
            m_old = m_s[h, at, :]
            m_new = jnp.maximum(m_old, top)
            keep = jnp.exp2((m_old - m_new) * EXP2_SCALE)
        p = jnp.exp2((s - m_new) * EXP2_SCALE)
        if rows == 256:
            p = jnp.concatenate([p[0:128] * mult, p[128:]], axis=0)
        elif mult is not None:
            p = p * mult
        total_p = jnp.sum(p, axis=1, keepdims=True)
        pv = jnp.dot(p.astype(BF16), values, preferred_element_type=F32)
        m_s[h, at, :] = m_new
        if fresh:
            l_s[h, at, :] = total_p
            acc_s[h, at, :] = pv
        else:
            l_s[h, at, :] = l_s[h, at, :] * keep + total_p
            acc_s[h, at, :] = acc_s[h, at, :] * keep + pv

    def full_head(zo, h, fresh=False):
        update(
            h, 0, 256, kv[zo, :, :, key_cols[h] : key_cols[h] + 128].reshape(256, 128),
            kv[zo, :, :, value_cols[h] : value_cols[h] + 128].reshape(256, 128), mask_s[h // 2], fresh,
        )

    def part_head(zo, h):
        update(
            h, 0, 128, kv[zo, :, 0:64, key_cols[h] : key_cols[h] + 128].reshape(128, 128),
            kv[zo, :, 0:64, value_cols[h] : value_cols[h] + 128].reshape(128, 128), low_mask_s[h // 2],
        )

    def pair_head(offsets, h):
        at = lambda e, col: c2[z_of[e], :, col : col + 128]
        update(
            h, 64 * (h // 2), 64, jnp.concatenate([at(e, key_cols[h]) for e in offsets], axis=0),
            jnp.concatenate([at(e, value_cols[h]) for e in offsets], axis=0), None,
        )

    tasks = []

    def run(count):
        for _ in range(min(count, len(tasks))):
            tasks.pop(0)()

    def heads(head, *args):
        for h in range(3):
            head(*args, h)

    def arrived(way, s):
        zo = origin(way, s + 1)
        if s == 3:
            pl.when(low_got(in_seg[way], s))(lambda: heads(part_head, zo))
        else:
            full = rest_got(in_seg[way], s)
            pl.when(full)(lambda: heads(full_head, zo))
            pl.when(jnp.logical_not(full))(lambda: heads(part_head, zo))

    def later(action, *args):
        tasks.append(lambda: action(*args))

    later(lambda: [full_head(z, h, fresh=True) for h in range(3)])
    for s in range(4):
        for k in (0, 1):
            run(1 if s else k)
            for way in (0, 1):
                take_piece(way, "low", s, k)
                if s < 3:
                    pass_on(way, "low", s + 1, k)
                to_pair(
                    origin(way, s + 1), k, "pair 0" if s < 2 else "pair 1",
                    None if s < 3 else low_got(in_seg[way], s),
                )
        if s < 3:
            for k in (0, 1):
                run(1 - k)
                for way in (0, 1):
                    take_piece(way, "rest", s, k)
                    if s < 2:
                        pass_on(way, "rest", s + 1, k)
        for way in (0, 1):
            later(arrived, way, s)
        if s == 2:
            take(c2.at[0:5], "pair 0")
            later(heads, pair_head, (0, 7, 1, 6, 2))
    run(len(tasks))
    take(c2.at[0:3], "pair 1")
    heads(pair_head, (3, 5, 4))

    heads = [acc_s[h] / l_s[h] for h in range(3)]
    done = jnp.concatenate(
        [jnp.where(lane256 < 64, heads[0], heads[1]), heads[2]], axis=1
    ).astype(BF16)
    def arranged(n):
        rows = jnp.dot(back_s[n], done, preferred_element_type=F32)
        a, b = rows[:, 0:128], rows[:, 128:256]
        a_rolled, b_rolled = roll64(a), roll64(b)
        return jnp.concatenate([
            jnp.where(c == 0, a, a_rolled),
            jnp.where(c == 0, b_rolled, b),
            jnp.where(c == 0, a_rolled, a),
        ], axis=1)

    fin[0] = arranged(0).astype(BF16)
    put(fin.at[0], fin.at[1], sibling, "fin", "fin")
    mine = arranged(1)
    take(fin.at[1], "fin")
    own_lane = (iota((128, HALF), 1) // 64) % 2 == c
    out_ref[...] = jnp.where(own_lane, mine, fin[1].astype(F32)).astype(BF16)

    for kind, ref in (
        ("z", wbuf.at[0, 0:4]), ("x", wbuf.at[0, 0:3]), ("cross", wbuf.at[0, 0, 0]), ("far", wbuf.at[0, 0:3]),
        ("bx", wbuf.at[0:3, 0:7, 0]), ("az", wbuf.at[0:3, 0:4, 0]), ("afar", wbuf.at[0:3, 0:3, 0]),
        ("pos", pos_sib), ("emb", emb_sib), ("mark x", marks_mid.at[0:3]), ("mark z", marks_got.at[0:7]),
        ("out x", xout), ("out z", got.at[0:7]), ("half", seqh.at[0]), ("fin", fin.at[0]),
        ("pair 0", c2.at[0:5]), ("pair 1", c2.at[0:3]),
    ):
        sent(ref, kind)
    for way in (0, 1):
        i = in_seg[way]
        sent(kv.at[0:3, :, 0:64], (way, "low"))
        sent(kv.at[0, :, 0:64], (way, "low", 3), low_sent(i, 3))
        for s in (0, 1, 2):
            sent(kv.at[0, :, 0:64], (way, "rest", s), rest_sent(i, s))
    assert len(names) <= N_SEMS, len(names)


def local(tile_embeddings, tile_position, input_weight, attention_weight):
    vmem = pl.BlockSpec(memory_space=pltpu.VMEM)
    anywhere = pl.BlockSpec(memory_space=pl.ANY)
    scratch = [
        pltpu.VMEM((1, SLOTS), jnp.int32),
        pltpu.VMEM((W_ROWS, 2 * HALF), BF16),
        pltpu.VMEM((SLOTS, E), BF16),
        pltpu.VMEM((SLOTS, E), BF16),
        pltpu.VMEM((1, SLOTS), jnp.int32),
        pltpu.VMEM((NX, NZ, 2, W_ROWS, HALF), BF16),
        pltpu.VMEM((D, 1152), BF16),
        pltpu.VMEM((D, 640), BF16),
        pltpu.VMEM((NX, NZ, 128), F32),
        pltpu.VMEM((NX, NZ, 128), F32),
        pltpu.VMEM((NZ, 8, 128), F32),
        pltpu.VMEM((NZ, 8, 128), F32),
        pltpu.VMEM((NX, 256, 2 * SLOTS), BF16),
        pltpu.VMEM((2 * SLOTS, HALF), BF16),
        pltpu.VMEM((NX, NZ, 2, 16, HALF), BF16),
        pltpu.VMEM((NZ, 2, NX, 16, HALF), BF16),
        pltpu.VMEM((3, NZ, 2, 16, HALF), BF16),
        pltpu.VMEM((NZ, 2, 128, HALF), BF16),
        pltpu.VMEM((NZ, 64, HALF), BF16),
        pltpu.VMEM((3, 256, 128), BF16),
        pltpu.VMEM((3, 256, 1), F32),
        pltpu.VMEM((3, 256, 1), F32),
        pltpu.VMEM((3, 256, 128), F32),
        pltpu.VMEM((2, 128, 256), F32),
        pltpu.VMEM((2, 128, 128), F32),
        pltpu.VMEM((2, 128, 512), BF16),
        pltpu.VMEM((2, 128, 256), BF16),
        pltpu.VMEM((2, 128, HALF), BF16),
        pltpu.VMEM((2, 2, 128, HALF), BF16),
        pltpu.SemaphoreType.DMA((N_SEMS,)),
        pltpu.SemaphoreType.DMA((4,)),
    ]
    return pl.pallas_call(
        kernel,
        out_shape=jax.ShapeDtypeStruct((TOK_DEV, HALF), BF16),
        in_specs=[anywhere] * 4,
        out_specs=vmem,
        scratch_shapes=scratch,
        compiler_params=pltpu.CompilerParams(
            collective_id=0, has_side_effects=True, vmem_limit_bytes=60 * 1024 * 1024
        ),
    )(tile_embeddings, tile_position.reshape(1, SLOTS), input_weight, attention_weight)


def solution(mesh):
    in_specs = (P(("slide", "seq"), None), P(("slide", "seq")), P("seq", None), P())
    out_specs = P(("slide", "seq"), None)
    return jax.shard_map(local, mesh=mesh, in_specs=in_specs, out_specs=out_specs, check_vma=False)
```
